512 devices in a mesh: row: 64 (over z, y), col: 8 (over x, core).
Axes of the slice: x: 4, y: 4, z: 16, core: 2. Of those that a mesh axis runs over, the one named last changes fastest.
Arguments:
- panel: float32 [131072, 256], P('row', 'col'), may hold values from -0.022097087 to 0.022097087, as said below
- trailing: float32 [131072, 2048], P('row', 'col'), may hold values from -6 to 6
Outputs:
- factor: float32 [256, 256], P(None, 'col')
- coupling: float32 [256, 2048], P(None, 'col')
- updated: float32 [131072, 2048], P('row', 'col')
The draws below stay inside these ranges and needn't reach their ends.
Inputs may be any that keep to these rules, and one draw needn't show every extreme that they name: A full-rank panel whose columns have norms of order one.
All inputs are finite; a program needn't handle non-finite values.
Results may differ from the reference program's by a relative error of at most 0.0003.
Values sent between devices are 32-bit elements; how exact they have to be, the bound alone decides.
A program may use at most 128 MiB of HBM per device.

```python
import jax
import jax.numpy as jnp
from jax import lax

PANEL = 256
TRAIL = 2048
ROWS = 131072


def draw_panel(key, part):
    key = jax.random.fold_in(key, 11)
    first, second, third = jax.random.split(key, 3)
    base = jax.random.truncated_normal(first, -6.0, 6.0, (ROWS, PANEL), jnp.float32)
    common = jax.random.truncated_normal(second, -6.0, 6.0, (ROWS, 1), jnp.float32)
    weights = jax.random.uniform(third, (1, PANEL), jnp.float32, -0.15, 0.15)
    values = base + weights * common
    values = values.at[0, 0].set(8.0).at[1, 1].set(-8.0)
    scale = 1.0 / jnp.sqrt(jnp.float32(ROWS))
    return (values * scale).astype(jnp.float32)


def block_levels(rng, dims, cuts, smallest, top_value):
    gain = 1.0
    for position, parts in cuts:
        draws = jax.random.uniform(jax.random.fold_in(jax.random.fold_in(rng, 6), position), (parts,), jnp.float32, smallest / len(cuts), top_value / len(cuts))
        gain = gain * jnp.repeat(jnp.exp(draws), dims[position] // parts).reshape((-1,) + (1,) * (len(dims) - 1 - position))
    return gain


def centred(own_key, shape, deviation, limit, cuts=(), kind=jnp.bfloat16):
    entries = deviation * jax.random.normal(own_key, shape, jnp.float32)
    if cuts:
        entries = entries * block_levels(own_key, shape, cuts, -0.22, 0.18)
    return jnp.clip(entries, -limit, limit).astype(kind)


def setup_inputs(seed: int = 0) -> dict:
    key_of = jax.random.split(jax.random.key(seed), 3)
    panel = draw_panel(jax.random.fold_in(key_of[2], 71), 0)
    trailing = centred(key_of[1], (ROWS, TRAIL), 1.0, 6.0, ((0, 64), (1, 8)), jnp.float32)
    return dict(panel=panel, trailing=trailing)


def reference(panel, trailing):
    ortho, upper = jnp.linalg.qr(panel)
    signs = jnp.sign(jnp.diagonal(upper))
    factor = upper * signs[:, None]
    cross = jnp.dot(panel.T.astype(jnp.float32), trailing.astype(jnp.float32), precision=lax.Precision.HIGHEST, preferred_element_type=jnp.float32)
    coupling = jax.scipy.linalg.solve_triangular(factor, cross, trans=1, lower=False)
    solved = jax.scipy.linalg.solve_triangular(factor, coupling, lower=False)
    updated = trailing - jnp.dot(panel.astype(jnp.float32), solved.astype(jnp.float32), precision=lax.Precision.HIGHEST, preferred_element_type=jnp.float32)
    return (factor, coupling, updated)
```

```python
import functools

import jax
import jax.numpy as jnp
from jax import lax
from jax.experimental import pallas as pl
from jax.experimental.pallas import tpu as pltpu
from jax.sharding import PartitionSpec as P

F32 = jnp.float32
BF16 = jnp.bfloat16
HIGHEST = lax.Precision.HIGHEST
MESH = pl.DeviceIdType.MESH
STEP = 16
LANES = 128


def split(value):
    high = value.astype(BF16)
    low = (value - high.astype(F32)).astype(BF16)
    return high, low


def dot3(left, right, dims):
    left_hi, left_lo = split(left)
    right_hi, right_lo = split(right)
    dot = functools.partial(
        lax.dot_general, dimension_numbers=(dims, ((), ())), preferred_element_type=F32
    )
    return dot(left_hi, right_hi) + (dot(left_hi, right_lo) + dot(left_lo, right_hi))


def remote(src, dst, send, recv, where):
    return pltpu.make_async_remote_copy(
        src_ref=src, dst_ref=dst, send_sem=send, recv_sem=recv, device_id=where, device_id_type=MESH
    )


def reduce_kernel(
    pt, tr, whole_out, gram_out, cross_out,
    whole, trail, gram_part, gram_y, gram_za, gram_zb, gram_full,
    cross_part, cross_y, cross_s, cross_z, cross_full,
    loc_sem, px_s, px_r, sb_s, sb_r, gy_s, gy_r, ga_s, ga_r, gb_s, gb_r, gf_s, gf_r,
    cy_s, cy_r, cz_s, cz_r, cg_s, cg_r, cf_s, cf_r,
):
    row, col = lax.axis_index("row"), lax.axis_index("col")
    z, y = row // 4, row % 4
    x, core = col // 2, col % 2
    zh, zl = z // 4, z % 4

    def at_y(d):
        return (z * 4 + (y + d) % 4, col)

    def at_z(d):
        return (((z + d) % 16) * 4 + y, col)

    def at_plane(d):
        spot = (y * 8 + col + d) % 32
        return (z * 4 + spot // 8, spot % 8)

    barrier = pltpu.get_barrier_semaphore()

    @pl.loop(1, 32)
    def _(d):
        pl.semaphore_signal(barrier, inc=1, device_id=at_plane(d), device_id_type=MESH)

    @pl.loop(1, 16)
    def _(d):
        pl.semaphore_signal(barrier, inc=1, device_id=at_z(d), device_id_type=MESH)

    pl.semaphore_wait(barrier, 46)

    half = pt.shape[1] // 2
    right, left = (row, ((x + 1) % 4) * 2 + core), (row, ((x + 3) % 4) * 2 + core)
    twin = (row, x * 2 + 1 - core)

    def slot(far, other, part):
        who = ((x + far) % 4) * 2 + (1 - core if other else core)
        return whole.at[pl.ds(pl.multiple_of(who * 32, 32), 32), pl.ds(part * half, half)]

    def own(part):
        return pt.at[:, pl.ds(part * half, half)]

    sends = {
        0: remote(own(0), slot(0, False, 0), px_s.at[0], px_r.at[0], right),
        1: remote(own(1), slot(0, False, 1), px_s.at[1], px_r.at[1], left),
        2: remote(own(1), slot(0, False, 1), px_s.at[2], px_r.at[2], right),
        3: remote(own(0), slot(0, False, 0), px_s.at[3], px_r.at[3], left),
    }
    for i in range(4):
        sends[i].start()
    to_twin = {}

    def relay(i, far, part, src=None):
        to_twin[i] = remote(
            slot(far, False, part) if src is None else src,
            slot(far, False, part), sb_s.at[i], sb_r.at[i], twin,
        )
        to_twin[i].start()

    relay(6, 0, 0, own(0))
    relay(7, 0, 1, own(1))
    mine = pltpu.make_async_copy(pt, whole.at[pl.ds(pl.multiple_of(col * 32, 32), 32), :], loc_sem.at[0])
    mine.start()
    load = pltpu.make_async_copy(tr, trail, loc_sem.at[1])
    load.start()

    sends[0].wait_recv()
    sends[4] = remote(slot(3, False, 0), slot(3, False, 0), px_s.at[4], px_r.at[4], right)
    sends[4].start()
    relay(0, 3, 0)
    sends[1].wait_recv()
    sends[5] = remote(slot(1, False, 1), slot(1, False, 1), px_s.at[5], px_r.at[5], left)
    sends[5].start()
    relay(1, 1, 1)
    sends[2].wait_recv()
    relay(2, 3, 1)
    sends[3].wait_recv()
    relay(3, 1, 0)
    sends[4].wait_recv()
    relay(4, 2, 0)
    sends[5].wait_recv()
    relay(5, 2, 1)
    mine.wait()
    load.wait()
    for i in range(8):
        to_twin[i].wait_recv()

    keep = pltpu.make_async_copy(whole, whole_out, loc_sem.at[2])
    keep.start()

    gram_part[...] = lax.dot_general(
        whole[pl.ds(pl.multiple_of(col * 32, 32), 32), :], whole[...],
        (((1,), (1,)), ((), ())), precision=HIGHEST, preferred_element_type=F32,
    )

    def eight(who):
        return pl.ds(pl.multiple_of(who * 8, 8), 8)

    def gram_y_copy(d):
        return remote(gram_part.at[eight((y + d) % 4)], gram_y.at[d], gy_s.at[d], gy_r.at[d], at_y(d))

    for d in range(1, 4):
        gram_y_copy(d).start()

    chunk = 512
    cross_part[...] = jnp.zeros_like(cross_part)

    @pl.loop(0, pt.shape[1] // chunk)
    def _(i):
        rows = pl.ds(pl.multiple_of(i * chunk, chunk), chunk)
        cross_part[...] += dot3(whole[:, rows], trail[rows, :], ((1,), (0,)))

    def cross_y_copy(d):
        return remote(
            cross_part.at[pl.ds(pl.multiple_of((y + d) % 4 * 64, 64), 64)], cross_y.at[d],
            cy_s.at[d], cy_r.at[d], at_y(d),
        )

    for d in range(1, 4):
        cross_y_copy(d).start()

    for d in range(1, 4):
        gram_y_copy(d).wait_recv()
    gram_za[zl] = gram_part[eight(y), :] + gram_y[1] + gram_y[2] + gram_y[3]

    def gram_za_copy(d):
        return remote(
            gram_za.at[zl], gram_za.at[zl], ga_s.at[d], ga_r.at[d],
            ((zh * 4 + (zl + d) % 4) * 4 + y, col),
        )

    def gram_za_recv(d):
        return remote(
            gram_za.at[zl], gram_za.at[(zl + 4 - d) % 4], ga_s.at[d], ga_r.at[d],
            ((zh * 4 + (zl + d) % 4) * 4 + y, col),
        )

    for d in range(1, 4):
        gram_za_copy(d).start()
    for d in range(1, 4):
        gram_za_recv(d).wait_recv()
    gram_zb[zh] = (gram_za[0] + gram_za[1]) + (gram_za[2] + gram_za[3])

    def gram_zb_copy(d, slot_of):
        return remote(
            gram_zb.at[zh], gram_zb.at[slot_of], gb_s.at[d], gb_r.at[d],
            ((((zh + d) % 4) * 4 + zl) * 4 + y, col),
        )

    for d in range(1, 4):
        gram_zb_copy(d, zh).start()

    for d in range(1, 4):
        cross_y_copy(d).wait_recv()
    own_rows = pl.ds(pl.multiple_of(y * 64, 64), 64)
    cross_s[...] = (cross_part[own_rows, :] + cross_y[1]) + (cross_y[2] + cross_y[3])

    def tile(ref, base, who):
        return ref.at[
            pl.ds(pl.multiple_of(base + who // 2 * 8, 8), 8),
            pl.ds(pl.multiple_of(who % 2 * LANES, LANES), LANES),
        ]

    def cross_z_copy(d):
        return remote(
            tile(cross_s, 0, (z + d) % 16), cross_z.at[d], cz_s.at[d], cz_r.at[d], at_z(d)
        )

    @pl.loop(1, 16)
    def _(d):
        cross_z_copy(d).start()

    for d in range(1, 4):
        gram_zb_copy(d, (zh + 4 - d) % 4).wait_recv()
    gram_full[eight(col * 4 + y), :] = (gram_zb[0] + gram_zb[1]) + (gram_zb[2] + gram_zb[3])

    def gram_f_copy(d, who):
        block = gram_full.at[eight(who)]
        return remote(gram_full.at[eight(col * 4 + y)], block, gf_s.at[d], gf_r.at[d], at_plane(d))

    @pl.loop(1, 32)
    def _(d):
        gram_f_copy(d, col * 4 + y).start()

    @pl.loop(1, 16)
    def _(d):
        cross_z_copy(d).wait_recv()

    mine_s = pl.ds(pl.multiple_of(z // 2 * 8, 8), 8)
    mine_l = pl.ds(pl.multiple_of(z % 2 * LANES, LANES), LANES)
    total = cross_s[mine_s, mine_l]
    for d in range(1, 16):
        total = total + cross_z[d]
    cross_full[pl.ds(pl.multiple_of(y * 64 + z // 2 * 8, 8), 8), mine_l] = total

    def cross_g_copy(d, who):
        return remote(
            tile(cross_full, y * 64, z), tile(cross_full, y * 64, who), cg_s.at[d], cg_r.at[d], at_z(d)
        )

    @pl.loop(1, 16)
    def _(d):
        cross_g_copy(d, z).start()

    @pl.loop(1, 32)
    def _(d):
        spot = (y * 8 + col + 32 - d) % 32
        gram_f_copy(d, spot % 8 * 4 + spot // 8).wait_recv()

    gram_out[...] = gram_full[...]

    @pl.loop(1, 16)
    def _(d):
        cross_g_copy(d, (z + 16 - d) % 16).wait_recv()

    def cross_f_copy(d, who):
        return remote(
            cross_full.at[own_rows], cross_full.at[pl.ds(pl.multiple_of(who * 64, 64), 64)],
            cf_s.at[d], cf_r.at[d], at_y(d),
        )

    for d in range(1, 4):
        cross_f_copy(d, y).start()
    for d in range(1, 4):
        cross_f_copy(d, (y + 4 - d) % 4).wait_recv()
    cross_out[...] = cross_full[...]

    keep.wait()
    for i in range(6):
        sends[i].wait_send()
    for i in range(8):
        to_twin[i].wait_send()
    for d in range(1, 4):
        gram_y_copy(d).wait_send()
        gram_za_copy(d).wait_send()
        gram_zb_copy(d, zh).wait_send()
        cross_y_copy(d).wait_send()
        cross_f_copy(d, y).wait_send()

    @pl.loop(1, 16)
    def _(d):
        cross_z_copy(d).wait_send()
        cross_g_copy(d, z).wait_send()

    @pl.loop(1, 32)
    def _(d):
        gram_f_copy(d, col * 4 + y).wait_send()


def factor_block(work, lower, index):
    order = work.shape[0]
    start = index * STEP
    upper_half = start < LANES
    places = [(work, 0), (work, 1), (lower, 0)] if upper_half else [(work, 1), (lower, 0), (lower, 1)]
    rows = [ref[start : start + STEP, LANES * q : LANES * (q + 1)] for ref, q in places]
    lane = start % LANES
    down = lax.broadcasted_iota(jnp.int32, (STEP, LANES), 0)
    columns = [jnp.broadcast_to(rows[0][:, lane + j : lane + j + 1], (STEP, LANES)) for j in range(STEP)]
    for j in range(STEP):
        scale = lax.rsqrt(columns[j][j : j + 1, :])
        below = jnp.where(down > j, columns[j] * scale, 0.0)
        for m in range(j + 1, STEP):
            columns[m] = columns[m] - below * below[m : m + 1, :]
        for q in range(3):
            pivot_row = rows[q][j : j + 1, :] * scale
            rows[q] = jnp.where(down == j, pivot_row, rows[q] - below * pivot_row)
    for (ref, q), value in zip(places, rows):
        ref[start : start + STEP, LANES * q : LANES * (q + 1)] = value
    if start + STEP < order:
        if upper_half:
            left = jnp.concatenate([rows[0], rows[1]], 1)[:, start + STEP :]
        else:
            left = rows[0][:, start + STEP - LANES :]
        update = lax.dot_general(
            left, jnp.concatenate(rows, 1), (((0,), (0,)), ((), ())),
            precision=HIGHEST, preferred_element_type=F32,
        )
        for i, (ref, q) in enumerate(places):
            ref[start + STEP :, LANES * q : LANES * (q + 1)] -= update[:, LANES * i : LANES * (i + 1)]


def solve_kernel(gram, cross, factor_out, coupling_out, solved_out, work, lower):
    order = gram.shape[0]
    across = lax.broadcasted_iota(jnp.int32, (order, order), 1)
    down = lax.broadcasted_iota(jnp.int32, (order, order), 0)
    work[...] = gram[...]
    lower[...] = jnp.where(down == across, 1.0, 0.0)
    for index in range(order // STEP):
        factor_block(work, lower, index)
    coupling = jnp.dot(lower[...], cross[...], precision=HIGHEST, preferred_element_type=F32)
    coupling_out[...] = coupling
    solved_out[...] = lax.dot_general(
        lower[...], coupling, (((0,), (0,)), ((), ())), precision=HIGHEST, preferred_element_type=F32
    )
    work[...] = jnp.where(across >= down, work[...], 0.0).T
    width = factor_out.shape[0]
    col = lax.axis_index("col")
    factor_out[...] = work[pl.ds(pl.multiple_of(col * width, width), width), :]


def reduce_call(pt, trailing):
    dma = pltpu.SemaphoreType.DMA
    rows = pt.shape[1]
    square = jax.ShapeDtypeStruct((256, 256), F32)
    vmem = pl.BlockSpec(memory_space=pltpu.VMEM)
    hbm = pl.BlockSpec(memory_space=pl.ANY)
    return pl.pallas_call(
        reduce_kernel,
        out_shape=(jax.ShapeDtypeStruct((256, rows), F32), square, square),
        in_specs=[hbm, hbm],
        out_specs=(hbm, vmem, vmem),
        scratch_shapes=[
            pltpu.VMEM((256, rows), F32),
            pltpu.VMEM(trailing.shape, F32),
            pltpu.VMEM((32, 256), F32),
            pltpu.VMEM((4, 8, 256), F32),
            pltpu.VMEM((4, 8, 256), F32),
            pltpu.VMEM((4, 8, 256), F32),
            pltpu.VMEM((256, 256), F32),
            pltpu.VMEM((256, 256), F32),
            pltpu.VMEM((4, 64, 256), F32),
            pltpu.VMEM((64, 256), F32),
            pltpu.VMEM((16, 8, LANES), F32),
            pltpu.VMEM((256, 256), F32),
            dma((3,)),
            dma((6,)), dma((6,)), dma((8,)), dma((8,)),
            dma((4,)), dma((4,)), dma((4,)), dma((4,)), dma((4,)), dma((4,)),
            dma((32,)), dma((32,)),
            dma((4,)), dma((4,)), dma((16,)), dma((16,)), dma((16,)), dma((16,)), dma((4,)), dma((4,)),
        ],
        compiler_params=pltpu.CompilerParams(
            collective_id=0, has_side_effects=True, vmem_limit_bytes=40 * 2**20
        ),
    )(pt, trailing)


def solve_call(gram, cross):
    square = jax.ShapeDtypeStruct((256, 256), F32)
    return pl.pallas_call(
        solve_kernel,
        out_shape=(jax.ShapeDtypeStruct((32, 256), F32), square, square),
        scratch_shapes=[pltpu.VMEM((256, 256), F32), pltpu.VMEM((256, 256), F32)],
        compiler_params=pltpu.CompilerParams(vmem_limit_bytes=16 * 2**20),
    )(gram, cross)


def on_device(panel, trailing):
    whole_t, gram, cross = reduce_call(panel.T, trailing)
    factor_t, coupling, solved = solve_call(gram, cross)
    updated = trailing - jnp.dot(
        whole_t.T, solved, precision=lax.Precision.HIGH, preferred_element_type=F32
    )
    return factor_t.T, coupling, updated


def solution(mesh):
    in_specs = (P("row", "col"), P("row", "col"))
    out_specs = (P(None, "col"), P(None, "col"), P("row", "col"))
    return jax.shard_map(
        on_device, mesh=mesh, in_specs=in_specs, out_specs=out_specs, check_vma=False
    )
```

```python
import functools

import jax
import jax.numpy as jnp
from jax import lax
from jax.experimental import pallas as pl
from jax.experimental.pallas import tpu as pltpu
from jax.sharding import PartitionSpec as P

F32 = jnp.float32
BF16 = jnp.bfloat16
HIGHEST = lax.Precision.HIGHEST
MESH = pl.DeviceIdType.MESH
STEP = 16
LANES = 128


def split(value):
    high = value.astype(BF16)
    low = (value - high.astype(F32)).astype(BF16)
    return high, low


def dot3(left, right, dims):
    left_hi, left_lo = split(left)
    right_hi, right_lo = split(right)
    dot = functools.partial(
        lax.dot_general, dimension_numbers=(dims, ((), ())), preferred_element_type=F32
    )
    return dot(left_hi, right_hi) + (dot(left_hi, right_lo) + dot(left_lo, right_hi))


def remote(src, dst, send, recv, where):
    return pltpu.make_async_remote_copy(
        src_ref=src, dst_ref=dst, send_sem=send, recv_sem=recv, device_id=where, device_id_type=MESH
    )


def total_of(parts):
    while len(parts) > 1:
        parts = [sum(parts[i : i + 2][1:], parts[i]) for i in range(0, len(parts), 2)]
    return parts[0]


def at(start, size):
    return pl.ds(pl.multiple_of(start * size, size), size)


def panel_kernel(
    pt, tr, whole_out, factor_out, coupling_out, solved_out,
    whole, trail, gram_part, gram_y, gram_z, gram_full,
    cross_part, cross_g, cross_z, cross_full, lower,
    loc_sem, px_s, px_r, sb_s, sb_r, gy_s, gy_r, gz_s, gz_r, gf_s, gf_r,
    cg_s, cg_r, cz_s, cz_r, cf_s, cf_r,
):
    row, col = lax.axis_index("row"), lax.axis_index("col")
    rem, div = lax.rem, lax.div
    z, y = div(row, 4), rem(row, 4)
    x, core = div(col, 2), rem(col, 2)
    zh, zl = div(z, 4), rem(z, 4)
    group = y * 4 + zl

    def at_y(d):
        return (z * 4 + rem(y + d, 4), col)

    def at_z(d):
        return (rem(z + d, 16) * 4 + y, col)

    def at_group(d):
        spot = rem(group + d, 16)
        return (zh * 16 + rem(spot, 4) * 4 + div(spot, 4), col)

    def at_plane(d):
        spot = rem(y * 8 + col + d, 32)
        return (z * 4 + div(spot, 8), rem(spot, 8))

    barrier = pltpu.get_barrier_semaphore()

    @pl.loop(1, 32)
    def _(d):
        pl.semaphore_signal(barrier, inc=1, device_id=at_plane(d), device_id_type=MESH)

    for d in range(1, 16):
        pl.semaphore_signal(barrier, inc=1, device_id=at_z(d), device_id_type=MESH)
    for dy in range(1, 4):
        for dz in range(1, 4):
            where = (zh * 16 + rem(zl + dz, 4) * 4 + rem(y + dy, 4), col)
            pl.semaphore_signal(barrier, inc=1, device_id=where, device_id_type=MESH)
    pl.semaphore_wait(barrier, 55)

    half = pt.shape[1] // 2
    right, left = (row, rem(x + 1, 4) * 2 + core), (row, rem(x + 3, 4) * 2 + core)
    twin = (row, x * 2 + 1 - core)

    def slot(far, part):
        return whole.at[at(rem(x + far, 4) * 2 + core, 32), pl.ds(part * half, half)]

    def own(part):
        return pt.at[:, pl.ds(part * half, half)]

    sends = {
        0: remote(own(0), slot(0, 0), px_s.at[0], px_r.at[0], right),
        1: remote(own(1), slot(0, 1), px_s.at[1], px_r.at[1], left),
        2: remote(own(1), slot(0, 1), px_s.at[2], px_r.at[2], right),
        3: remote(own(0), slot(0, 0), px_s.at[3], px_r.at[3], left),
    }
    for i in range(4):
        sends[i].start()
    to_twin = {}

    def relay(i, far, part, src=None):
        to_twin[i] = remote(
            slot(far, part) if src is None else src, slot(far, part), sb_s.at[i], sb_r.at[i], twin
        )
        to_twin[i].start()

    relay(6, 0, 0, own(0))
    relay(7, 0, 1, own(1))
    mine = pltpu.make_async_copy(pt, whole.at[at(col, 32), :], loc_sem.at[0])
    mine.start()
    load = pltpu.make_async_copy(tr, trail, loc_sem.at[1])
    load.start()

    sends[0].wait_recv()
    sends[4] = remote(slot(3, 0), slot(3, 0), px_s.at[4], px_r.at[4], right)
    sends[4].start()
    relay(0, 3, 0)
    sends[1].wait_recv()
    sends[5] = remote(slot(1, 1), slot(1, 1), px_s.at[5], px_r.at[5], left)
    sends[5].start()
    relay(1, 1, 1)
    sends[2].wait_recv()
    relay(2, 3, 1)
    sends[3].wait_recv()
    relay(3, 1, 0)
    sends[4].wait_recv()
    relay(4, 2, 0)
    sends[5].wait_recv()
    relay(5, 2, 1)
    mine.wait()
    load.wait()
    for i in range(8):
        to_twin[i].wait_recv()

    gram_part[...] = lax.dot_general(
        whole[at(col, 32), :], whole[...],
        (((1,), (1,)), ((), ())), precision=HIGHEST, preferred_element_type=F32,
    )

    def gram_y_copy(d):
        return remote(gram_part.at[at(rem(y + d, 4), 8)], gram_y.at[d], gy_s.at[d], gy_r.at[d], at_y(d))

    for d in (2, 1, 3):
        gram_y_copy(d).start()

    keep = pltpu.make_async_copy(whole, whole_out, loc_sem.at[2])
    keep.start()
    chunk = 512
    cross_part[...] = jnp.zeros_like(cross_part)

    @pl.loop(0, pt.shape[1] // chunk)
    def _(i):
        cross_part[...] += dot3(whole[:, at(i, chunk)], trail[at(i, chunk), :], ((1,), (0,)))

    def cross_g_copy(d):
        return remote(
            cross_part.at[at(rem(group + d, 16), 16)], cross_g.at[d], cg_s.at[d], cg_r.at[d], at_group(d)
        )

    @pl.loop(1, 16)
    def _(d):
        cross_g_copy(d).start()

    for d in range(1, 4):
        gram_y_copy(d).wait_recv()
    gram_z[z] = (gram_part[at(y, 8), :] + gram_y[1]) + (gram_y[2] + gram_y[3])

    def gram_z_copy(d, who):
        return remote(gram_z.at[z], gram_z.at[who], gz_s.at[d], gz_r.at[d], at_z(d))

    for d in (8, 7, 9, 6, 10, 5, 11, 4, 12, 3, 13, 2, 14, 1, 15):
        gram_z_copy(d, z).start()

    @pl.loop(1, 16)
    def _(d):
        cross_g_copy(d).wait_recv()

    cross_z[zh] = total_of([cross_part[at(group, 16), :]] + [cross_g[d] for d in range(1, 16)])

    def cross_z_copy(d, who):
        where = (rem(z + 4 * d, 16) * 4 + y, col)
        return remote(cross_z.at[zh], cross_z.at[who], cz_s.at[d], cz_r.at[d], where)

    for d in (2, 1, 3):
        cross_z_copy(d, zh).start()

    for d in range(1, 16):
        gram_z_copy(d, rem(z + 16 - d, 16)).wait_recv()
    gram_full[at(col * 4 + y, 8), :] = total_of([gram_z[i] for i in range(16)])

    def gram_f_copy(d, who):
        return remote(
            gram_full.at[at(col * 4 + y, 8)], gram_full.at[at(who, 8)], gf_s.at[d], gf_r.at[d], at_plane(d)
        )

    @pl.loop(1, 32)
    def _(d):
        gram_f_copy(d, col * 4 + y).start()

    for d in range(1, 4):
        cross_z_copy(d, rem(zh + 4 - d, 4)).wait_recv()
    cross_full[at(group, 16), :] = total_of([cross_z[i] for i in range(4)])

    def cross_f_copy(d, who):
        return remote(
            cross_full.at[at(group, 16)], cross_full.at[at(who, 16)], cf_s.at[d], cf_r.at[d], at_group(d)
        )

    @pl.loop(1, 16)
    def _(d):
        cross_f_copy(d, group).start()

    @pl.loop(1, 32)
    def _(d):
        spot = rem(y * 8 + col + 32 - d, 32)
        gram_f_copy(d, rem(spot, 8) * 4 + div(spot, 8)).wait_recv()

    @pl.loop(1, 32)
    def _(d):
        gram_f_copy(d, col * 4 + y).wait_send()

    order = gram_full.shape[0]
    across = lax.broadcasted_iota(jnp.int32, (order, order), 1)
    down = lax.broadcasted_iota(jnp.int32, (order, order), 0)
    lower[...] = jnp.where(down == across, 1.0, 0.0)
    for index in range(order // STEP):
        factor_block(gram_full, lower, index)

    @pl.loop(1, 16)
    def _(d):
        cross_f_copy(d, rem(group + 16 - d, 16)).wait_recv()

    coupling = jnp.dot(lower[...], cross_full[...], precision=HIGHEST, preferred_element_type=F32)
    coupling_out[...] = coupling
    solved_out[...] = lax.dot_general(
        lower[...], coupling, (((0,), (0,)), ((), ())), precision=HIGHEST, preferred_element_type=F32
    )
    gram_full[...] = jnp.where(across >= down, gram_full[...], 0.0).T
    factor_out[...] = gram_full[at(col, 32), :]

    keep.wait()
    for i in range(6):
        sends[i].wait_send()
    for i in range(8):
        to_twin[i].wait_send()
    for d in range(1, 4):
        gram_y_copy(d).wait_send()
        cross_z_copy(d, zh).wait_send()

    @pl.loop(1, 16)
    def _(d):
        gram_z_copy(d, z).wait_send()
        cross_g_copy(d).wait_send()
        cross_f_copy(d, group).wait_send()


def factor_block(work, lower, index):
    order = work.shape[0]
    start = index * STEP
    upper_half = start < LANES
    places = [(work, 0), (work, 1), (lower, 0)] if upper_half else [(work, 1), (lower, 0), (lower, 1)]
    rows = jnp.concatenate([ref[start : start + STEP, LANES * q : LANES * (q + 1)] for ref, q in places], 1)
    lane = start % LANES
    down = lax.broadcasted_iota(jnp.int32, (STEP, LANES), 0)
    wide = lax.broadcasted_iota(jnp.int32, rows.shape, 0)
    columns = [jnp.broadcast_to(rows[:, lane + j : lane + j + 1], (STEP, LANES)) for j in range(STEP)]
    for j in range(STEP):
        scale = lax.rsqrt(columns[j][j : j + 1, :])
        below = jnp.where(down > j, columns[j] * scale, 0.0)
        for m in range(j + 1, STEP):
            columns[m] = columns[m] - below * below[m : m + 1, :]
        pivot_row = rows[j : j + 1, :] * jnp.concatenate([scale] * 3, 1)
        rows = jnp.where(wide == j, pivot_row, rows - jnp.concatenate([below] * 3, 1) * pivot_row)
    for i, (ref, q) in enumerate(places):
        ref[start : start + STEP, LANES * q : LANES * (q + 1)] = rows[:, LANES * i : LANES * (i + 1)]
    if start + STEP < order:
        left = rows[:, start + STEP : 2 * LANES] if upper_half else rows[:, start + STEP - LANES : LANES]
        update = lax.dot_general(
            left, rows, (((0,), (0,)), ((), ())), precision=HIGHEST, preferred_element_type=F32
        )
        for i, (ref, q) in enumerate(places):
            ref[start + STEP :, LANES * q : LANES * (q + 1)] -= update[:, LANES * i : LANES * (i + 1)]


def panel_call(pt, trailing):
    dma = pltpu.SemaphoreType.DMA
    rows = pt.shape[1]
    square = jax.ShapeDtypeStruct((256, 256), F32)
    vmem = pl.BlockSpec(memory_space=pltpu.VMEM)
    hbm = pl.BlockSpec(memory_space=pltpu.HBM)
    return pl.pallas_call(
        panel_kernel,
        out_shape=(
            jax.ShapeDtypeStruct((256, rows), F32), jax.ShapeDtypeStruct((32, 256), F32), square, square,
        ),
        in_specs=[hbm, hbm],
        out_specs=(pl.BlockSpec(memory_space=pl.ANY), vmem, vmem, vmem),
        scratch_shapes=[
            pltpu.VMEM((256, rows), F32),
            pltpu.VMEM(trailing.shape, F32),
            pltpu.VMEM((32, 256), F32),
            pltpu.VMEM((4, 8, 256), F32),
            pltpu.VMEM((16, 8, 256), F32),
            pltpu.VMEM((256, 256), F32),
            pltpu.VMEM((256, 256), F32),
            pltpu.VMEM((16, 16, 256), F32),
            pltpu.VMEM((4, 16, 256), F32),
            pltpu.VMEM((256, 256), F32),
            pltpu.VMEM((256, 256), F32),
            dma((3,)),
            dma((6,)), dma((6,)), dma((8,)), dma((8,)),
            dma((4,)), dma((4,)), dma((16,)), dma((16,)), dma((32,)), dma((32,)),
            dma((16,)), dma((16,)), dma((4,)), dma((4,)), dma((16,)), dma((16,)),
        ],
        compiler_params=pltpu.CompilerParams(
            collective_id=0, has_side_effects=True, vmem_limit_bytes=40 * 2**20
        ),
    )(pltpu.with_memory_space_constraint(pt, pltpu.HBM), pltpu.with_memory_space_constraint(trailing, pltpu.HBM))


def on_device(panel, trailing):
    whole_t, factor_t, coupling, solved = panel_call(panel.T, trailing)
    updated = trailing - jnp.dot(
        whole_t.T, solved, precision=lax.Precision.HIGH, preferred_element_type=F32
    )
    return factor_t.T, coupling, updated


def solution(mesh):
    in_specs = (P("row", "col"), P("row", "col"))
    out_specs = (P(None, "col"), P(None, "col"), P("row", "col"))
    return jax.shard_map(
        on_device, mesh=mesh, in_specs=in_specs, out_specs=out_specs, check_vma=False
    )
```

```python
import functools

import jax
import jax.numpy as jnp
from jax import lax
from jax.experimental import pallas as pl
from jax.experimental.pallas import tpu as pltpu
from jax.sharding import PartitionSpec as P

F32 = jnp.float32
BF16 = jnp.bfloat16
HIGHEST = lax.Precision.HIGHEST
MESH = pl.DeviceIdType.MESH
STEP = 16
LANES = 128


def split(value):
    high = value.astype(BF16)
    low = (value - high.astype(F32)).astype(BF16)
    return high, low


def dot3(left, right, dims):
    left_hi, left_lo = split(left)
    right_hi, right_lo = split(right)
    dot = functools.partial(
        lax.dot_general, dimension_numbers=(dims, ((), ())), preferred_element_type=F32
    )
    return dot(left_hi, right_hi) + (dot(left_hi, right_lo) + dot(left_lo, right_hi))


def remote(src, dst, send, recv, where):
    return pltpu.make_async_remote_copy(
        src_ref=src, dst_ref=dst, send_sem=send, recv_sem=recv, device_id=where, device_id_type=MESH
    )


def total_of(parts):
    while len(parts) > 1:
        parts = [sum(parts[i : i + 2][1:], parts[i]) for i in range(0, len(parts), 2)]
    return parts[0]


def at(start, size):
    return pl.ds(pl.multiple_of(start * size, size), size)


def panel_kernel(
    pt, tr, whole_out, upper_out, lower_out, cross_out,
    whole, trail, slab, gram_part, gram_p, gram_z, gram_full,
    cross_part, cross_g, cross_z, cross_full, lower,
    loc_sem, ps_s, ps_r, px_s, px_r, sb_s, sb_r, gp_s, gp_r, gz_s, gz_r, gf_s, gf_r,
    cg_s, cg_r, cz_s, cz_r, cf_s, cf_r,
):
    row, col = lax.axis_index("row"), lax.axis_index("col")
    rem, div = lax.rem, lax.div
    z, y = div(row, 4), rem(row, 4)
    x, core = div(col, 2), rem(col, 2)
    zh, zl = div(z, 4), rem(z, 4)
    group = y * 4 + zl

    def at_z(d):
        return (rem(z + d, 16) * 4 + y, col)

    def at_group(d):
        spot = rem(group + d, 16)
        return (zh * 16 + rem(spot, 4) * 4 + div(spot, 4), col)

    mine = y * 8 + col

    def at_plane(d):
        spot = rem(mine + d, 32)
        return (z * 4 + div(spot, 8), rem(spot, 8))

    far_first = (8, 7, 9, 6, 10, 5, 11, 4, 12, 3, 13, 2, 14, 1, 15)
    barrier = pltpu.get_barrier_semaphore()
    for d in far_first:
        pl.semaphore_signal(barrier, inc=1, device_id=at_z(d), device_id_type=MESH)
    for dy in range(1, 4):
        for dz in range(1, 4):
            where = (zh * 16 + rem(zl + dz, 4) * 4 + rem(y + dy, 4), col)
            pl.semaphore_signal(barrier, inc=1, device_id=where, device_id_type=MESH)

    @pl.loop(1, 32)
    def _(d):
        pl.semaphore_signal(barrier, inc=1, device_id=at_plane(d), device_id_type=MESH)

    pl.semaphore_wait(barrier, 55)

    def slab_copy(d):
        who = rem(col + d, 8)
        return remote(pt.at[:, at(who, 256)], slab.at[at(col, 32)], ps_s.at[d], ps_r.at[d], (row, who))

    def slab_recv(d):
        who = rem(col + d, 8)
        return remote(
            pt.at[:, at(who, 256)], slab.at[at(rem(col + 8 - d, 8), 32)], ps_s.at[d], ps_r.at[d], (row, who)
        )

    for d in (4, 3, 5, 2, 6, 1, 7):
        slab_copy(d).start()
    slab_own = pltpu.make_async_copy(pt.at[:, at(col, 256)], slab.at[at(col, 32)], loc_sem.at[3])
    slab_own.start()

    half = pt.shape[1] // 2
    right, left = (row, rem(x + 1, 4) * 2 + core), (row, rem(x + 3, 4) * 2 + core)
    twin = (row, x * 2 + 1 - core)

    def slot(far, part):
        return whole.at[at(rem(x + far, 4) * 2 + core, 32), pl.ds(part * half, half)]

    def own(part):
        return pt.at[:, pl.ds(part * half, half)]

    sends = {
        0: remote(own(0), slot(0, 0), px_s.at[0], px_r.at[0], right),
        1: remote(own(1), slot(0, 1), px_s.at[1], px_r.at[1], left),
        2: remote(own(1), slot(0, 1), px_s.at[2], px_r.at[2], right),
        3: remote(own(0), slot(0, 0), px_s.at[3], px_r.at[3], left),
    }
    for i in range(4):
        sends[i].start()
    to_twin = {}

    def relay(i, far, part, src=None):
        to_twin[i] = remote(
            slot(far, part) if src is None else src, slot(far, part), sb_s.at[i], sb_r.at[i], twin
        )
        to_twin[i].start()

    relay(6, 0, 0, own(0))
    relay(7, 0, 1, own(1))
    panel_own = pltpu.make_async_copy(pt, whole.at[at(col, 32), :], loc_sem.at[0])
    panel_own.start()
    load = pltpu.make_async_copy(tr, trail, loc_sem.at[1])
    load.start()

    slab_own.wait()
    for d in range(1, 8):
        slab_recv(d).wait_recv()
    gram_part[...] = lax.dot_general(
        slab[...], slab[...], (((1,), (1,)), ((), ())), precision=HIGHEST, preferred_element_type=F32
    )

    def gram_p_copy(d):
        return remote(
            gram_part.at[at(rem(mine + d, 32), 8)], gram_p.at[d], gp_s.at[d], gp_r.at[d], at_plane(d)
        )

    @pl.loop(1, 32)
    def _(d):
        gram_p_copy(d).start()

    sends[0].wait_recv()
    sends[4] = remote(slot(3, 0), slot(3, 0), px_s.at[4], px_r.at[4], right)
    sends[4].start()
    relay(0, 3, 0)
    sends[1].wait_recv()
    sends[5] = remote(slot(1, 1), slot(1, 1), px_s.at[5], px_r.at[5], left)
    sends[5].start()
    relay(1, 1, 1)
    sends[2].wait_recv()
    relay(2, 3, 1)
    sends[3].wait_recv()
    relay(3, 1, 0)

    @pl.loop(1, 32)
    def _(d):
        gram_p_copy(d).wait_recv()

    gram_z[z] = total_of([gram_part[at(mine, 8), :]] + [gram_p[d] for d in range(1, 32)])

    def gram_z_copy(d, who):
        return remote(gram_z.at[z], gram_z.at[who], gz_s.at[d], gz_r.at[d], at_z(d))

    for d in far_first:
        gram_z_copy(d, z).start()

    sends[4].wait_recv()
    relay(4, 2, 0)
    sends[5].wait_recv()
    relay(5, 2, 1)
    panel_own.wait()
    load.wait()
    for i in range(8):
        to_twin[i].wait_recv()

    keep = pltpu.make_async_copy(whole, whole_out, loc_sem.at[2])
    keep.start()
    chunk = 512
    cross_part[...] = jnp.zeros_like(cross_part)

    @pl.loop(0, pt.shape[1] // chunk)
    def _(i):
        cross_part[...] += dot3(whole[:, at(i, chunk)], trail[at(i, chunk), :], ((1,), (0,)))

    def cross_g_copy(d):
        return remote(
            cross_part.at[at(rem(group + d, 16), 16)], cross_g.at[d], cg_s.at[d], cg_r.at[d], at_group(d)
        )

    @pl.loop(1, 16)
    def _(d):
        cross_g_copy(d).start()

    for d in range(1, 16):
        gram_z_copy(d, rem(z + 16 - d, 16)).wait_recv()
    gram_full[at(mine, 8), :] = total_of([gram_z[i] for i in range(16)])

    def gram_f_copy(d, who):
        return remote(
            gram_full.at[at(mine, 8)], gram_full.at[at(who, 8)], gf_s.at[d], gf_r.at[d], at_plane(d)
        )

    @pl.loop(1, 32)
    def _(d):
        gram_f_copy(d, mine).start()

    @pl.loop(1, 16)
    def _(d):
        cross_g_copy(d).wait_recv()

    cross_z[zh] = total_of([cross_part[at(group, 16), :]] + [cross_g[d] for d in range(1, 16)])

    def cross_z_copy(d, who):
        where = (rem(z + 4 * d, 16) * 4 + y, col)
        return remote(cross_z.at[zh], cross_z.at[who], cz_s.at[d], cz_r.at[d], where)

    for d in (2, 1, 3):
        cross_z_copy(d, zh).start()

    @pl.loop(1, 32)
    def _(d):
        gram_f_copy(d, rem(mine + 32 - d, 32)).wait_recv()

    @pl.loop(1, 32)
    def _(d):
        gram_f_copy(d, mine).wait_send()

    order = gram_full.shape[0]
    across = lax.broadcasted_iota(jnp.int32, (order, order), 1)
    down = lax.broadcasted_iota(jnp.int32, (order, order), 0)
    lower[...] = jnp.where(down == across, 1.0, 0.0)
    for index in range(order // STEP // 2):
        factor_block(gram_full, lower, index)

    for d in range(1, 4):
        cross_z_copy(d, rem(zh + 4 - d, 4)).wait_recv()
    cross_full[at(group, 16), :] = total_of([cross_z[i] for i in range(4)])

    def cross_f_copy(d, who):
        return remote(
            cross_full.at[at(group, 16)], cross_full.at[at(who, 16)], cf_s.at[d], cf_r.at[d], at_group(d)
        )

    @pl.loop(1, 16)
    def _(d):
        cross_f_copy(d, group).start()

    for index in range(order // STEP // 2, order // STEP):
        factor_block(gram_full, lower, index)

    @pl.loop(1, 16)
    def _(d):
        cross_f_copy(d, rem(group + 16 - d, 16)).wait_recv()

    upper_out[...] = gram_full[...]
    lower_out[...] = lower[...]
    cross_out[...] = cross_full[...]

    keep.wait()
    for i in range(6):
        sends[i].wait_send()
    for i in range(8):
        to_twin[i].wait_send()
    for d in range(1, 4):
        cross_z_copy(d, zh).wait_send()

    @pl.loop(1, 16)
    def _(d):
        gram_z_copy(d, z).wait_send()
        cross_g_copy(d).wait_send()
        cross_f_copy(d, group).wait_send()

    for d in range(1, 8):
        slab_copy(d).wait_send()

    @pl.loop(1, 32)
    def _(d):
        gram_p_copy(d).wait_send()


def factor_block(work, lower, index):
    order = work.shape[0]
    start = index * STEP
    upper_half = start < LANES
    places = [(work, 0), (work, 1), (lower, 0)] if upper_half else [(work, 1), (lower, 0), (lower, 1)]
    rows = jnp.concatenate([ref[start : start + STEP, LANES * q : LANES * (q + 1)] for ref, q in places], 1)
    lane = start % LANES
    down = lax.broadcasted_iota(jnp.int32, (STEP, LANES), 0)
    wide = lax.broadcasted_iota(jnp.int32, rows.shape, 0)
    columns = [jnp.broadcast_to(rows[:, lane + j : lane + j + 1], (STEP, LANES)) for j in range(STEP)]
    for j in range(STEP):
        scale = lax.rsqrt(columns[j][j : j + 1, :])
        below = jnp.where(down > j, columns[j] * scale, 0.0)
        for m in range(j + 1, STEP):
            columns[m] = columns[m] - below * below[m : m + 1, :]
        pivot_row = rows[j : j + 1, :] * jnp.concatenate([scale] * 3, 1)
        rows = jnp.where(wide == j, pivot_row, rows - jnp.concatenate([below] * 3, 1) * pivot_row)
    for i, (ref, q) in enumerate(places):
        ref[start : start + STEP, LANES * q : LANES * (q + 1)] = rows[:, LANES * i : LANES * (i + 1)]
    if start + STEP < order:
        left = rows[:, start + STEP : 2 * LANES] if upper_half else rows[:, start + STEP - LANES : LANES]
        update = lax.dot_general(
            left, rows, (((0,), (0,)), ((), ())), precision=HIGHEST, preferred_element_type=F32
        )
        for i, (ref, q) in enumerate(places):
            ref[start + STEP :, LANES * q : LANES * (q + 1)] -= update[:, LANES * i : LANES * (i + 1)]


def panel_call(pt, trailing):
    dma = pltpu.SemaphoreType.DMA
    rows = pt.shape[1]
    square = jax.ShapeDtypeStruct((256, 256), F32)
    vmem = pl.BlockSpec(memory_space=pltpu.VMEM)
    hbm = pl.BlockSpec(memory_space=pltpu.HBM)
    return pl.pallas_call(
        panel_kernel,
        out_shape=(
            jax.ShapeDtypeStruct((256, rows), F32), square, square, square,
        ),
        in_specs=[hbm, hbm],
        out_specs=(pl.BlockSpec(memory_space=pl.ANY), vmem, vmem, vmem),
        scratch_shapes=[
            pltpu.VMEM((256, rows), F32),
            pltpu.VMEM(trailing.shape, F32),
            pltpu.VMEM((256, 256), F32),
            pltpu.VMEM((256, 256), F32),
            pltpu.VMEM((32, 8, 256), F32),
            pltpu.VMEM((16, 8, 256), F32),
            pltpu.VMEM((256, 256), F32),
            pltpu.VMEM((256, 256), F32),
            pltpu.VMEM((16, 16, 256), F32),
            pltpu.VMEM((4, 16, 256), F32),
            pltpu.VMEM((256, 256), F32),
            pltpu.VMEM((256, 256), F32),
            dma((4,)), dma((8,)), dma((8,)),
            dma((6,)), dma((6,)), dma((8,)), dma((8,)),
            dma((32,)), dma((32,)), dma((16,)), dma((16,)), dma((32,)), dma((32,)),
            dma((16,)), dma((16,)), dma((4,)), dma((4,)), dma((16,)), dma((16,)),
        ],
        compiler_params=pltpu.CompilerParams(
            collective_id=0, has_side_effects=True, vmem_limit_bytes=40 * 2**20
        ),
    )(pltpu.with_memory_space_constraint(pt, pltpu.HBM), pltpu.with_memory_space_constraint(trailing, pltpu.HBM))


def update_kernel(whole, upper, lower, cross, trail, factor_out, coupling_out, updated_out, scratch, block, sems):
    order = upper.shape[0]
    across = lax.broadcasted_iota(jnp.int32, (order, order), 1)
    down = lax.broadcasted_iota(jnp.int32, (order, order), 0)
    coupling = jnp.dot(lower[...], cross[...], precision=HIGHEST, preferred_element_type=F32)
    coupling_out[...] = coupling
    solved = lax.dot_general(
        lower[...], coupling, (((0,), (0,)), ((), ())), precision=HIGHEST, preferred_element_type=F32
    )
    steps, size = block.shape[0], block.shape[1]
    copies = []
    for i in range(steps):
        rows = slice(i * size, (i + 1) * size)
        block[i] = trail[rows, :] - dot3(whole[:, rows], solved, ((0,), (0,)))
        copies.append(pltpu.make_async_copy(block.at[i], updated_out.at[pl.ds(i * size, size)], sems.at[i]))
        copies[-1].start()
    scratch[...] = jnp.where(across >= down, upper[...], 0.0).T
    factor_out[...] = scratch[at(lax.axis_index("col"), 32), :]
    for copy in copies:
        copy.wait()


def update_call(whole_t, upper, lower, cross, trailing):
    rows, width = trailing.shape
    vmem = pl.BlockSpec(memory_space=pltpu.VMEM)
    steps = 8
    return pl.pallas_call(
        update_kernel,
        out_shape=(
            jax.ShapeDtypeStruct((32, 256), F32), jax.ShapeDtypeStruct((256, width), F32),
            jax.ShapeDtypeStruct((rows, width), F32),
        ),
        in_specs=[vmem] * 5,
        out_specs=(vmem, vmem, pl.BlockSpec(memory_space=pl.ANY)),
        scratch_shapes=[
            pltpu.VMEM((256, 256), F32),
            pltpu.VMEM((steps, rows // steps, width), F32),
            pltpu.SemaphoreType.DMA((steps,)),
        ],
        compiler_params=pltpu.CompilerParams(vmem_limit_bytes=40 * 2**20),
    )(whole_t, upper, lower, cross, trailing)


def on_device(panel, trailing):
    whole_t, upper, lower, cross = panel_call(panel.T, trailing)
    factor_t, coupling, updated = update_call(whole_t, upper, lower, cross, trailing)
    return factor_t.T, coupling, updated


def solution(mesh):
    in_specs = (P("row", "col"), P("row", "col"))
    out_specs = (P(None, "col"), P(None, "col"), P("row", "col"))
    return jax.shard_map(
        on_device, mesh=mesh, in_specs=in_specs, out_specs=out_specs, check_vma=False
    )
```

```python
import functools

import jax
import jax.numpy as jnp
from jax import lax
from jax.experimental import pallas as pl
from jax.experimental.pallas import tpu as pltpu
from jax.sharding import PartitionSpec as P

F32 = jnp.float32
BF16 = jnp.bfloat16
HIGHEST = lax.Precision.HIGHEST
MESH = pl.DeviceIdType.MESH
STEP = 16
LANES = 128


def split(value):
    high = value.astype(BF16)
    low = (value - high.astype(F32)).astype(BF16)
    return high, low


def dot3(left, right, dims):
    left_hi, left_lo = split(left)
    right_hi, right_lo = split(right)
    dot = functools.partial(
        lax.dot_general, dimension_numbers=(dims, ((), ())), preferred_element_type=F32
    )
    return dot(left_hi, right_hi) + (dot(left_hi, right_lo) + dot(left_lo, right_hi))


def remote(src, dst, send, recv, where):
    return pltpu.make_async_remote_copy(
        src_ref=src, dst_ref=dst, send_sem=send, recv_sem=recv, device_id=where, device_id_type=MESH
    )


def total_of(parts):
    while len(parts) > 1:
        parts = [sum(parts[i : i + 2][1:], parts[i]) for i in range(0, len(parts), 2)]
    return parts[0]


def at(start, size):
    return pl.ds(pl.multiple_of(start * size, size), size)


def panel_kernel(
    pt, tr, whole_out, upper_out, lower_out, cross_out,
    whole, trail, trail_hi, trail_lo, slab, gram_part, gram_p, gram_z, gram_full,
    cross_part, cross_g, cross_z, cross_full, lower,
    loc_sem, ps_s, ps_r, px_s, px_r, sb_s, sb_r, gp_s, gp_r, gz_s, gz_r, gf_s, gf_r,
    cg_s, cg_r, cz_s, cz_r, cf_s, cf_r,
):
    row, col = lax.axis_index("row"), lax.axis_index("col")
    rem, div = lax.rem, lax.div
    z, y = div(row, 4), rem(row, 4)
    x, core = div(col, 2), rem(col, 2)
    zh, zl = div(z, 4), rem(z, 4)
    ys = [y] + [rem(y + d, 4) for d in range(1, 4)]
    cols = [col] + [rem(col + d, 8) for d in range(1, 8)]
    zs = [z] + [rem(z + d, 16) for d in range(1, 16)]
    near = [zl] + [rem(zl + d, 4) for d in range(1, 4)]
    chips = [x] + [rem(x + d, 4) for d in range(1, 4)]

    plane = [(dy, dc) for dy in (2, 1, 3, 0) for dc in (4, 3, 5, 2, 6, 1, 7, 0) if (dy, dc) != (0, 0)]
    block = [(dy, dz) for dz in (2, 1, 3, 0) for dy in (2, 1, 3, 0) if (dy, dz) != (0, 0)]
    line = (8, 7, 9, 6, 10, 5, 11, 4, 12, 3, 13, 2, 14, 1, 15)

    def at_plane(dy, dc):
        return (z * 4 + ys[dy], cols[dc])

    def at_z(d):
        return (zs[d] * 4 + y, col)

    def at_block(dy, dz):
        return (zh * 16 + near[dz] * 4 + ys[dy], col)

    barrier = pltpu.get_barrier_semaphore()
    for d in line:
        pl.semaphore_signal(barrier, inc=1, device_id=at_z(d), device_id_type=MESH)
    for dy, dz in block:
        if dy and dz:
            pl.semaphore_signal(barrier, inc=1, device_id=at_block(dy, dz), device_id_type=MESH)
    for dy, dc in plane:
        pl.semaphore_signal(barrier, inc=1, device_id=at_plane(dy, dc), device_id_type=MESH)
    pl.semaphore_wait(barrier, 55)

    def slab_copy(d, who):
        return remote(
            pt.at[:, at(cols[d], 256)], slab.at[at(who, 32)], ps_s.at[d], ps_r.at[d], (row, cols[d])
        )

    for d in (4, 3, 5, 2, 6, 1, 7):
        slab_copy(d, col).start()
    slab_own = pltpu.make_async_copy(pt.at[:, at(col, 256)], slab.at[at(col, 32)], loc_sem.at[3])
    slab_own.start()

    half = pt.shape[1] // 2
    right, left = (row, chips[1] * 2 + core), (row, chips[3] * 2 + core)
    twin = (row, x * 2 + 1 - core)

    def slot(far, part):
        return whole.at[at(chips[far] * 2 + core, 32), pl.ds(part * half, half)]

    def own(part):
        return pt.at[:, pl.ds(part * half, half)]

    sends = {
        0: remote(own(0), slot(0, 0), px_s.at[0], px_r.at[0], right),
        1: remote(own(1), slot(0, 1), px_s.at[1], px_r.at[1], left),
        2: remote(own(1), slot(0, 1), px_s.at[2], px_r.at[2], right),
        3: remote(own(0), slot(0, 0), px_s.at[3], px_r.at[3], left),
    }
    for i in range(4):
        sends[i].start()
    to_twin = {}

    def relay(i, far, part, src=None):
        to_twin[i] = remote(
            slot(far, part) if src is None else src, slot(far, part), sb_s.at[i], sb_r.at[i], twin
        )
        to_twin[i].start()

    relay(6, 0, 0, own(0))
    relay(7, 0, 1, own(1))
    panel_own = pltpu.make_async_copy(pt, whole.at[at(col, 32), :], loc_sem.at[0])
    panel_own.start()
    load = pltpu.make_async_copy(tr, trail, loc_sem.at[1])
    load.start()

    load.wait()
    chunk = 256

    @pl.loop(0, pt.shape[1] // chunk)
    def _(i):
        high, low = split(trail[at(i, chunk), :])
        trail_hi[at(i, chunk), :] = high
        trail_lo[at(i, chunk), :] = low

    slab_own.wait()
    for d in range(1, 8):
        slab_copy(d, cols[8 - d]).wait_recv()
    gram_part[...] = lax.dot_general(
        slab[...], slab[...], (((1,), (1,)), ((), ())), precision=HIGHEST, preferred_element_type=F32
    )
    mine = y * 8 + col

    def gram_p_copy(dy, dc):
        d = dy * 8 + dc
        return remote(
            gram_part.at[at(ys[dy] * 8 + cols[dc], 8)], gram_p.at[d], gp_s.at[d], gp_r.at[d], at_plane(dy, dc)
        )

    for dy, dc in plane:
        gram_p_copy(dy, dc).start()

    sends[0].wait_recv()
    sends[4] = remote(slot(3, 0), slot(3, 0), px_s.at[4], px_r.at[4], right)
    sends[4].start()
    relay(0, 3, 0)
    sends[1].wait_recv()
    sends[5] = remote(slot(1, 1), slot(1, 1), px_s.at[5], px_r.at[5], left)
    sends[5].start()
    relay(1, 1, 1)

    def cross_g_copy(dy, dz):
        d = dy * 4 + dz
        return remote(
            cross_part.at[at(ys[dy] * 4 + near[dz], 16)], cross_g.at[d], cg_s.at[d], cg_r.at[d], at_block(dy, dz)
        )

    def cross_stage(far):
        rows = at(chips[far], 64)
        high, low = split(whole[rows, :])
        dot = functools.partial(jnp.dot, preferred_element_type=F32)
        cross_part[rows, :] = dot(high, trail_hi[...]) + (
            dot(high, trail_lo[...]) + dot(low, trail_hi[...])
        )
        for dy in range(4):

            @pl.when(ys[dy] == chips[far])
            def _():
                for dz in (2, 1, 3, 0):
                    if dy or dz:
                        cross_g_copy(dy, dz).start()

    panel_own.wait()
    to_twin[6].wait_recv()
    to_twin[7].wait_recv()
    cross_stage(0)
    sends[2].wait_recv()
    relay(2, 3, 1)
    sends[3].wait_recv()
    relay(3, 1, 0)

    for dy, dc in plane:
        gram_p_copy(dy, dc).wait_recv()
    gram_z[z] = total_of([gram_part[at(mine, 8), :]] + [gram_p[d] for d in range(1, 32)])

    def gram_z_copy(d, who):
        return remote(gram_z.at[z], gram_z.at[who], gz_s.at[d], gz_r.at[d], at_z(d))

    for d in line:
        gram_z_copy(d, z).start()

    sends[4].wait_recv()
    relay(4, 2, 0)
    sends[5].wait_recv()
    relay(5, 2, 1)
    for i in range(4):
        to_twin[i].wait_recv()
    cross_stage(1)
    cross_stage(3)
    to_twin[4].wait_recv()
    to_twin[5].wait_recv()
    cross_stage(2)
    keep = pltpu.make_async_copy(whole, whole_out, loc_sem.at[2])
    keep.start()

    group = y * 4 + zl
    for dy, dz in block:
        cross_g_copy(dy, dz).wait_recv()
    cross_z[zh] = total_of([cross_part[at(group, 16), :]] + [cross_g[d] for d in range(1, 16)])

    def cross_z_copy(d, who):
        return remote(cross_z.at[zh], cross_z.at[who], cz_s.at[d], cz_r.at[d], at_z(4 * d))

    for d in (2, 1, 3):
        cross_z_copy(d, zh).start()

    for d in range(1, 16):
        gram_z_copy(d, zs[16 - d]).wait_recv()
    gram_full[at(mine, 8), :] = total_of([gram_z[i] for i in range(16)])

    def gram_f_copy(dy, dc, who):
        d = dy * 8 + dc
        return remote(
            gram_full.at[at(mine, 8)], gram_full.at[at(who, 8)], gf_s.at[d], gf_r.at[d], at_plane(dy, dc)
        )

    for dy, dc in plane:
        gram_f_copy(dy, dc, mine).start()

    for dy, dc in plane:
        gram_f_copy(dy, dc, ys[-dy] * 8 + cols[-dc]).wait_recv()

    for dy, dc in plane:
        gram_f_copy(dy, dc, mine).wait_send()

    order = gram_full.shape[0]
    across = lax.broadcasted_iota(jnp.int32, (order, order), 1)
    down = lax.broadcasted_iota(jnp.int32, (order, order), 0)
    lower[...] = jnp.where(down == across, 1.0, 0.0)
    early = 2
    for index in range(early):
        factor_block(gram_full, lower, index)

    for d in range(1, 4):
        cross_z_copy(d, rem(zh + 4 - d, 4)).wait_recv()
    cross_full[at(group, 16), :] = total_of([cross_z[i] for i in range(4)])

    def cross_f_copy(dy, dz, who):
        d = dy * 4 + dz
        return remote(
            cross_full.at[at(group, 16)], cross_full.at[at(who, 16)], cf_s.at[d], cf_r.at[d], at_block(dy, dz)
        )

    for dy, dz in block:
        cross_f_copy(dy, dz, group).start()

    for index in range(early, order // STEP):
        factor_block(gram_full, lower, index)

    for dy, dz in block:
        cross_f_copy(dy, dz, ys[-dy] * 4 + near[-dz]).wait_recv()

    upper_out[...] = gram_full[...]
    lower_out[...] = lower[...]
    cross_out[...] = cross_full[...]

    keep.wait()
    for i in range(6):
        sends[i].wait_send()
    for i in range(8):
        to_twin[i].wait_send()
    for d in range(1, 4):
        cross_z_copy(d, zh).wait_send()
    for d in range(1, 16):
        gram_z_copy(d, z).wait_send()
    for dy, dz in block:
        cross_g_copy(dy, dz).wait_send()
        cross_f_copy(dy, dz, group).wait_send()
    for d in range(1, 8):
        slab_copy(d, col).wait_send()
    for dy, dc in plane:
        gram_p_copy(dy, dc).wait_send()


def factor_block(work, lower, index):
    order = work.shape[0]
    start = index * STEP
    upper_half = start < LANES
    places = [(work, 0), (work, 1), (lower, 0)] if upper_half else [(work, 1), (lower, 0), (lower, 1)]
    rows = jnp.concatenate([ref[start : start + STEP, LANES * q : LANES * (q + 1)] for ref, q in places], 1)
    lane = start % LANES
    down = lax.broadcasted_iota(jnp.int32, (STEP, LANES), 0)
    wide = lax.broadcasted_iota(jnp.int32, rows.shape, 0)
    columns = [jnp.broadcast_to(rows[:, lane + j : lane + j + 1], (STEP, LANES)) for j in range(STEP)]
    for j in range(STEP):
        scale = lax.rsqrt(columns[j][j : j + 1, :])
        below = jnp.where(down > j, columns[j] * scale, 0.0)
        for m in range(j + 1, STEP):
            columns[m] = columns[m] - below * below[m : m + 1, :]
        pivot_row = rows[j : j + 1, :] * jnp.concatenate([scale] * 3, 1)
        rows = jnp.where(wide == j, pivot_row, rows - jnp.concatenate([below] * 3, 1) * pivot_row)
    for i, (ref, q) in enumerate(places):
        ref[start : start + STEP, LANES * q : LANES * (q + 1)] = rows[:, LANES * i : LANES * (i + 1)]
    if start + STEP < order:
        left = rows[:, start + STEP : 2 * LANES] if upper_half else rows[:, start + STEP - LANES : LANES]
        update = lax.dot_general(
            left, rows, (((0,), (0,)), ((), ())), precision=HIGHEST, preferred_element_type=F32
        )
        for i, (ref, q) in enumerate(places):
            ref[start + STEP :, LANES * q : LANES * (q + 1)] -= update[:, LANES * i : LANES * (i + 1)]


def panel_call(pt, trailing):
    dma = pltpu.SemaphoreType.DMA
    rows = pt.shape[1]
    square = jax.ShapeDtypeStruct((256, 256), F32)
    vmem = pl.BlockSpec(memory_space=pltpu.VMEM)
    hbm = pl.BlockSpec(memory_space=pltpu.HBM)
    return pl.pallas_call(
        panel_kernel,
        out_shape=(
            jax.ShapeDtypeStruct((256, rows), F32), square, square, square,
        ),
        in_specs=[hbm, hbm],
        out_specs=(pl.BlockSpec(memory_space=pl.ANY), vmem, vmem, vmem),
        scratch_shapes=[
            pltpu.VMEM((256, rows), F32),
            pltpu.VMEM(trailing.shape, F32),
            pltpu.VMEM(trailing.shape, BF16),
            pltpu.VMEM(trailing.shape, BF16),
            pltpu.VMEM((256, 256), F32),
            pltpu.VMEM((256, 256), F32),
            pltpu.VMEM((32, 8, 256), F32),
            pltpu.VMEM((16, 8, 256), F32),
            pltpu.VMEM((256, 256), F32),
            pltpu.VMEM((256, 256), F32),
            pltpu.VMEM((16, 16, 256), F32),
            pltpu.VMEM((4, 16, 256), F32),
            pltpu.VMEM((256, 256), F32),
            pltpu.VMEM((256, 256), F32),
            dma((4,)), dma((8,)), dma((8,)),
            dma((6,)), dma((6,)), dma((8,)), dma((8,)),
            dma((32,)), dma((32,)), dma((16,)), dma((16,)), dma((32,)), dma((32,)),
            dma((16,)), dma((16,)), dma((4,)), dma((4,)), dma((16,)), dma((16,)),
        ],
        compiler_params=pltpu.CompilerParams(
            collective_id=0, has_side_effects=True, vmem_limit_bytes=40 * 2**20
        ),
    )(pltpu.with_memory_space_constraint(pt, pltpu.HBM), pltpu.with_memory_space_constraint(trailing, pltpu.HBM))


def update_kernel(whole, upper, lower, cross, trail, factor_out, coupling_out, updated_out, scratch, block, sems):
    order = upper.shape[0]
    across = lax.broadcasted_iota(jnp.int32, (order, order), 1)
    down = lax.broadcasted_iota(jnp.int32, (order, order), 0)
    coupling = jnp.dot(lower[...], cross[...], precision=HIGHEST, preferred_element_type=F32)
    coupling_out[...] = coupling
    solved = lax.dot_general(
        lower[...], coupling, (((0,), (0,)), ((), ())), precision=HIGHEST, preferred_element_type=F32
    )
    steps, size = block.shape[0], block.shape[1]
    copies = []
    for i in range(steps):
        rows = slice(i * size, (i + 1) * size)
        block[i] = trail[rows, :] - dot3(whole[:, rows], solved, ((0,), (0,)))
        copies.append(pltpu.make_async_copy(block.at[i], updated_out.at[pl.ds(i * size, size)], sems.at[i]))
        copies[-1].start()
    scratch[...] = jnp.where(across >= down, upper[...], 0.0).T
    factor_out[...] = scratch[at(lax.axis_index("col"), 32), :]
    for copy in copies:
        copy.wait()


def update_call(whole_t, upper, lower, cross, trailing):
    rows, width = trailing.shape
    vmem = pl.BlockSpec(memory_space=pltpu.VMEM)
    steps = 8
    return pl.pallas_call(
        update_kernel,
        out_shape=(
            jax.ShapeDtypeStruct((32, 256), F32), jax.ShapeDtypeStruct((256, width), F32),
            jax.ShapeDtypeStruct((rows, width), F32),
        ),
        in_specs=[vmem] * 5,
        out_specs=(vmem, vmem, pl.BlockSpec(memory_space=pl.ANY)),
        scratch_shapes=[
            pltpu.VMEM((256, 256), F32),
            pltpu.VMEM((steps, rows // steps, width), F32),
            pltpu.SemaphoreType.DMA((steps,)),
        ],
        compiler_params=pltpu.CompilerParams(vmem_limit_bytes=40 * 2**20),
    )(whole_t, upper, lower, cross, trailing)


def on_device(panel, trailing):
    whole_t, upper, lower, cross = panel_call(panel.T, trailing)
    factor_t, coupling, updated = update_call(whole_t, upper, lower, cross, trailing)
    return factor_t.T, coupling, updated


def solution(mesh):
    in_specs = (P("row", "col"), P("row", "col"))
    out_specs = (P(None, "col"), P(None, "col"), P("row", "col"))
    return jax.shard_map(
        on_device, mesh=mesh, in_specs=in_specs, out_specs=out_specs, check_vma=False
    )
```

```python
import functools

import jax
import jax.numpy as jnp
from jax import lax
from jax.experimental import pallas as pl
from jax.experimental.pallas import tpu as pltpu
from jax.sharding import PartitionSpec as P

F32 = jnp.float32
BF16 = jnp.bfloat16
HIGHEST = lax.Precision.HIGHEST
MESH = pl.DeviceIdType.MESH
STEP = 32
LANES = 128


def split(value):
    high = value.astype(BF16)
    low = (value - high.astype(F32)).astype(BF16)
    return high, low


def dot3(left, right, dims):
    left_hi, left_lo = split(left)
    right_hi, right_lo = split(right)
    dot = functools.partial(
        lax.dot_general, dimension_numbers=(dims, ((), ())), preferred_element_type=F32
    )
    return dot(left_hi, right_hi) + (dot(left_hi, right_lo) + dot(left_lo, right_hi))


def remote(src, dst, send, recv, where):
    return pltpu.make_async_remote_copy(
        src_ref=src, dst_ref=dst, send_sem=send, recv_sem=recv, device_id=where, device_id_type=MESH
    )


def total_of(parts):
    while len(parts) > 1:
        parts = [sum(parts[i : i + 2][1:], parts[i]) for i in range(0, len(parts), 2)]
    return parts[0]


def at(start, size):
    return pl.ds(pl.multiple_of(start * size, size), size)


def panel_kernel(
    pt, tr, whole_out, work, cross_out,
    whole, trail, trail_hi, trail_lo, slab, gram_part, gram_t, gram_p, gram_z, gram_full,
    cross_part, cross_g, cross_z, cross_full,
    loc_sem, ps_s, ps_r, px_s, px_r, sb_s, sb_r, gp_s, gp_r, gz_s, gz_r, gf_s, gf_r,
    tw_s, tw_r, cg_s, cg_r, cz_s, cz_r, cf_s, cf_r,
):
    row, col = lax.axis_index("row"), lax.axis_index("col")
    rem, div = lax.rem, lax.div
    z, y = div(row, 4), rem(row, 4)
    x, core = div(col, 2), rem(col, 2)
    zh, zl = div(z, 4), rem(z, 4)
    ys = [y] + [rem(y + d, 4) for d in range(1, 4)]
    cols = [col] + [rem(col + d, 8) for d in range(1, 8)]
    zs = [z] + [rem(z + d, 16) for d in range(1, 16)]
    near = [zl] + [rem(zl + d, 4) for d in range(1, 4)]
    chips = [x] + [rem(x + d, 4) for d in range(1, 4)]

    plane = [(dy, dx) for dy in (2, 1, 3, 0) for dx in (2, 1, 3, 0) if (dy, dx) != (0, 0)]
    block = [(dy, dz) for dz in (2, 1, 3, 0) for dy in (2, 1, 3, 0) if (dy, dz) != (0, 0)]
    line = (8, 7, 9, 6, 10, 5, 11, 4, 12, 3, 13, 2, 14, 1, 15)

    def at_plane(dy, dx):
        return (z * 4 + ys[dy], chips[dx] * 2 + core)

    def at_z(d):
        return (zs[d] * 4 + y, col)

    def at_block(dy, dz):
        return (zh * 16 + near[dz] * 4 + ys[dy], col)

    barrier = pltpu.get_barrier_semaphore()
    for d in line:
        pl.semaphore_signal(barrier, inc=1, device_id=at_z(d), device_id_type=MESH)
    for dy, dz in block:
        if dy and dz:
            pl.semaphore_signal(barrier, inc=1, device_id=at_block(dy, dz), device_id_type=MESH)
    for dy, dx in plane:
        pl.semaphore_signal(barrier, inc=1, device_id=at_plane(dy, dx), device_id_type=MESH)
    for dx in (2, 1, 3, 0):
        where = (row, chips[dx] * 2 + 1 - core)
        pl.semaphore_signal(barrier, inc=1, device_id=where, device_id_type=MESH)
    pl.semaphore_wait(barrier, 43)

    def slab_copy(d, who):
        return remote(
            pt.at[:, at(cols[d], 256)], slab.at[at(who, 32)], ps_s.at[d], ps_r.at[d], (row, cols[d])
        )

    for d in (4, 3, 5, 2, 6, 1, 7):
        slab_copy(d, col).start()
    slab_own = pltpu.make_async_copy(pt.at[:, at(col, 256)], slab.at[at(col, 32)], loc_sem.at[3])
    slab_own.start()

    half = pt.shape[1] // 2
    right, left = (row, chips[1] * 2 + core), (row, chips[3] * 2 + core)
    twin = (row, x * 2 + 1 - core)

    def slot(far, part):
        return whole.at[at(chips[far] * 2 + core, 32), pl.ds(part * half, half)]

    def own(part):
        return pt.at[:, pl.ds(part * half, half)]

    sends = {
        0: remote(own(0), slot(0, 0), px_s.at[0], px_r.at[0], right),
        1: remote(own(1), slot(0, 1), px_s.at[1], px_r.at[1], left),
        2: remote(own(1), slot(0, 1), px_s.at[2], px_r.at[2], right),
        3: remote(own(0), slot(0, 0), px_s.at[3], px_r.at[3], left),
    }
    for i in range(4):
        sends[i].start()
    to_twin = {}

    def relay(i, far, part, src=None):
        to_twin[i] = remote(
            slot(far, part) if src is None else src, slot(far, part), sb_s.at[i], sb_r.at[i], twin
        )
        to_twin[i].start()

    relay(6, 0, 0, own(0))
    relay(7, 0, 1, own(1))
    panel_own = pltpu.make_async_copy(pt, whole.at[at(col, 32), :], loc_sem.at[0])
    panel_own.start()
    load = pltpu.make_async_copy(tr, trail, loc_sem.at[1])
    load.start()

    load.wait()
    chunk = 256

    @pl.loop(0, pt.shape[1] // chunk)
    def _(i):
        high, low = split(trail[at(i, chunk), :])
        trail_hi[at(i, chunk), :] = high
        trail_lo[at(i, chunk), :] = low

    slab_own.wait()
    for d in range(1, 8):
        slab_copy(d, cols[8 - d]).wait_recv()
    gram_part[...] = lax.dot_general(
        slab[...], slab[...], (((1,), (1,)), ((), ())), precision=HIGHEST, preferred_element_type=F32
    )
    gram_twin = remote(gram_part.at[at(1 - core, 128)], gram_t, tw_s.at[0], tw_r.at[0], twin)
    gram_twin.start()
    gram_twin.wait_recv()
    gram_t[...] += gram_part[at(core, 128), :]
    place = y * 4 + x
    mine = core * 16 + place

    def gram_p_copy(dy, dx):
        d = dy * 4 + dx
        return remote(
            gram_t.at[at(ys[dy] * 4 + chips[dx], 8)], gram_p.at[d], gp_s.at[d], gp_r.at[d], at_plane(dy, dx)
        )

    for dy, dx in plane:
        gram_p_copy(dy, dx).start()

    sends[0].wait_recv()
    sends[4] = remote(slot(3, 0), slot(3, 0), px_s.at[4], px_r.at[4], right)
    sends[4].start()
    relay(0, 3, 0)
    sends[1].wait_recv()
    sends[5] = remote(slot(1, 1), slot(1, 1), px_s.at[5], px_r.at[5], left)
    sends[5].start()
    relay(1, 1, 1)

    def cross_g_copy(dy, dz):
        d = dy * 4 + dz
        return remote(
            cross_part.at[at(ys[dy] * 4 + near[dz], 16)], cross_g.at[d], cg_s.at[d], cg_r.at[d], at_block(dy, dz)
        )

    def cross_stage(far):
        rows = at(chips[far], 64)
        high, low = split(whole[rows, :])
        dot = functools.partial(jnp.dot, preferred_element_type=F32)
        cross_part[rows, :] = dot(high, trail_hi[...]) + (
            dot(high, trail_lo[...]) + dot(low, trail_hi[...])
        )
        for dy in range(4):

            @pl.when(ys[dy] == chips[far])
            def _():
                for dz in (2, 1, 3, 0):
                    if dy or dz:
                        cross_g_copy(dy, dz).start()

    panel_own.wait()
    to_twin[6].wait_recv()
    to_twin[7].wait_recv()
    cross_stage(0)
    sends[2].wait_recv()
    relay(2, 3, 1)
    sends[3].wait_recv()
    relay(3, 1, 0)

    for dy, dx in plane:
        gram_p_copy(dy, dx).wait_recv()
    gram_z[z] = total_of([gram_t[at(place, 8), :]] + [gram_p[d] for d in range(1, 16)])

    def gram_z_copy(d, who):
        return remote(gram_z.at[z], gram_z.at[who], gz_s.at[d], gz_r.at[d], at_z(d))

    for d in line:
        gram_z_copy(d, z).start()

    sends[4].wait_recv()
    relay(4, 2, 0)
    sends[5].wait_recv()
    relay(5, 2, 1)
    for i in range(4):
        to_twin[i].wait_recv()
    cross_stage(1)
    cross_stage(3)
    to_twin[4].wait_recv()
    to_twin[5].wait_recv()
    cross_stage(2)
    keep = pltpu.make_async_copy(whole, whole_out, loc_sem.at[2])
    keep.start()

    group = y * 4 + zl
    for d in range(1, 16):
        gram_z_copy(d, zs[16 - d]).wait_recv()
    gram_full[at(mine, 8), :] = total_of([gram_z[i] for i in range(16)])

    def gram_f_copy(dy, dx, who):
        d = dy * 4 + dx
        return remote(
            gram_full.at[at(mine, 8)], gram_full.at[at(who, 8)], gf_s.at[d], gf_r.at[d], at_plane(dy, dx)
        )

    for dy, dx in plane:
        gram_f_copy(dy, dx, mine).start()

    for dy, dz in block:
        cross_g_copy(dy, dz).wait_recv()
    cross_z[zh] = total_of([cross_part[at(group, 16), :]] + [cross_g[d] for d in range(1, 16)])

    def cross_z_copy(d, who):
        return remote(cross_z.at[zh], cross_z.at[who], cz_s.at[d], cz_r.at[d], at_z(4 * d))

    for d in (2, 1, 3):
        cross_z_copy(d, zh).start()

    for dy, dx in plane:
        gram_f_copy(dy, dx, core * 16 + ys[-dy] * 4 + chips[-dx]).wait_recv()

    def full_twin(who):
        rows = gram_full.at[at(who, 128)]
        return remote(gram_full.at[at(core, 128)], rows, tw_s.at[1], tw_r.at[1], twin)

    full_twin(core).start()
    full_twin(1 - core).wait_recv()

    def cross_f_copy(dy, dz, who):
        d = dy * 4 + dz
        return remote(
            cross_full.at[at(group, 16)], cross_full.at[at(who, 16)], cf_s.at[d], cf_r.at[d], at_block(dy, dz)
        )

    def share_cross():
        for d in range(1, 4):
            cross_z_copy(d, rem(zh + 4 - d, 4)).wait_recv()
        cross_full[at(group, 16), :] = total_of([cross_z[i] for i in range(4)])
        for dy, dz in block:
            cross_f_copy(dy, dz, group).start()

    factor(gram_full, work, share_cross)

    for dy, dz in block:
        cross_f_copy(dy, dz, ys[-dy] * 4 + near[-dz]).wait_recv()
    cross_out[...] = cross_full[...]

    keep.wait()
    for i in range(6):
        sends[i].wait_send()
    for i in range(8):
        to_twin[i].wait_send()
    for d in range(1, 4):
        cross_z_copy(d, zh).wait_send()
    for d in range(1, 16):
        gram_z_copy(d, z).wait_send()
    for dy, dz in block:
        cross_g_copy(dy, dz).wait_send()
        cross_f_copy(dy, dz, group).wait_send()
    for d in range(1, 8):
        slab_copy(d, col).wait_send()
    for dy, dx in plane:
        gram_p_copy(dy, dx).wait_send()
        gram_f_copy(dy, dx, mine).wait_send()
    gram_twin.wait_send()
    full_twin(core).wait_send()


def eliminate(rows, lane):
    down = lax.broadcasted_iota(jnp.int32, (STEP, LANES), 0)
    wide = lax.broadcasted_iota(jnp.int32, rows.shape, 0)
    columns = [jnp.broadcast_to(rows[:, lane + j : lane + j + 1], (STEP, LANES)) for j in range(STEP)]

    def across(value):
        return jnp.concatenate([value] * 3, 1)

    for j in range(0, STEP, 2):
        first, second = columns[j][j : j + 1, :], columns[j][j + 1 : j + 2, :]
        third = columns[j + 1][j + 1 : j + 2, :]
        scale_0 = lax.rsqrt(first)
        scale_1 = lax.rsqrt(first * third - second * second) * (first * scale_0)
        link = second * scale_0
        below_0 = jnp.where(down > j, columns[j] * scale_0, 0.0)
        below_1 = jnp.where(down > j + 1, (columns[j + 1] - below_0 * link) * scale_1, 0.0)
        for m in range(j + 2, STEP):
            columns[m] = columns[m] - (below_0 * below_0[m : m + 1, :] + below_1 * below_1[m : m + 1, :])
        row_0 = rows[j : j + 1, :] * across(scale_0)
        row_1 = (rows[j + 1 : j + 2, :] - across(link) * row_0) * across(scale_1)
        rest = rows - (across(below_0) * row_0 + across(below_1) * row_1)
        rows = jnp.where(wide == j, row_0, jnp.where(wide == j + 1, row_1, rest))
    return rows


def factor(gram, work, midway):
    order = gram.shape[0]
    work[...] = jnp.zeros_like(work)

    def span(start):
        return (0, 3 * LANES) if start < LANES else (LANES, 4 * LANES)

    def base(start):
        across = lax.broadcasted_iota(jnp.int32, (STEP, order), 1)
        down = lax.broadcasted_iota(jnp.int32, (STEP, order), 0)
        unit = jnp.where(across == down + start, 1.0, 0.0)
        low, high = span(start)
        return jnp.concatenate([gram[start : start + STEP, :], unit], 1)[:, low:high]

    def terms(start, first, last):
        low, high = span(start)
        return lax.dot_general(
            work[first:last, start : start + STEP], work[first:last, low:high],
            (((0,), (0,)), ((), ())), precision=HIGHEST, preferred_element_type=F32,
        )

    ready = base(0)
    for start in range(0, order, STEP):
        later = start + STEP
        if later < order:
            ahead = base(later)
            if start:
                ahead = ahead - terms(later, 0, start)
        low, high = span(start)
        work[start:later, low:high] = eliminate(ready, start % LANES)
        if start == 0:
            midway()
        if later < order:
            ready = ahead - terms(later, start, later)


def panel_call(pt, trailing):
    dma = pltpu.SemaphoreType.DMA
    rows = pt.shape[1]
    square = jax.ShapeDtypeStruct((256, 256), F32)
    vmem = pl.BlockSpec(memory_space=pltpu.VMEM)
    hbm = pl.BlockSpec(memory_space=pltpu.HBM)
    return pl.pallas_call(
        panel_kernel,
        out_shape=(
            jax.ShapeDtypeStruct((256, rows), F32), jax.ShapeDtypeStruct((256, 512), F32), square,
        ),
        in_specs=[hbm, hbm],
        out_specs=(pl.BlockSpec(memory_space=pl.ANY), vmem, vmem),
        scratch_shapes=[
            pltpu.VMEM((256, rows), F32),
            pltpu.VMEM(trailing.shape, F32),
            pltpu.VMEM(trailing.shape, BF16),
            pltpu.VMEM(trailing.shape, BF16),
            pltpu.VMEM((256, 256), F32),
            pltpu.VMEM((256, 256), F32),
            pltpu.VMEM((128, 256), F32),
            pltpu.VMEM((16, 8, 256), F32),
            pltpu.VMEM((16, 8, 256), F32),
            pltpu.VMEM((256, 256), F32),
            pltpu.VMEM((256, 256), F32),
            pltpu.VMEM((16, 16, 256), F32),
            pltpu.VMEM((4, 16, 256), F32),
            pltpu.VMEM((256, 256), F32),
            dma((4,)), dma((8,)), dma((8,)),
            dma((6,)), dma((6,)), dma((8,)), dma((8,)),
            dma((16,)), dma((16,)), dma((16,)), dma((16,)), dma((16,)), dma((16,)), dma((2,)), dma((2,)),
            dma((16,)), dma((16,)), dma((4,)), dma((4,)), dma((16,)), dma((16,)),
        ],
        compiler_params=pltpu.CompilerParams(
            collective_id=0, has_side_effects=True, vmem_limit_bytes=40 * 2**20
        ),
    )(pltpu.with_memory_space_constraint(pt, pltpu.HBM), pltpu.with_memory_space_constraint(trailing, pltpu.HBM))


def update_kernel(whole, work, cross, trail, factor_out, coupling_out, updated_out, scratch, block, sems):
    order = work.shape[0]
    upper, lower = work[:, :order], work[:, order:]
    across = lax.broadcasted_iota(jnp.int32, (order, order), 1)
    down = lax.broadcasted_iota(jnp.int32, (order, order), 0)
    coupling = jnp.dot(lower, cross[...], precision=HIGHEST, preferred_element_type=F32)
    coupling_out[...] = coupling
    solved = lax.dot_general(
        lower, coupling, (((0,), (0,)), ((), ())), precision=HIGHEST, preferred_element_type=F32
    )
    steps, size = block.shape[0], block.shape[1]
    copies = []
    for i in range(steps):
        rows = slice(i * size, (i + 1) * size)
        block[i] = trail[rows, :] - dot3(whole[:, rows], solved, ((0,), (0,)))
        copies.append(pltpu.make_async_copy(block.at[i], updated_out.at[pl.ds(i * size, size)], sems.at[i]))
        copies[-1].start()
    scratch[...] = jnp.where(across >= down, upper, 0.0).T
    factor_out[...] = scratch[at(lax.axis_index("col"), 32), :]
    for copy in copies:
        copy.wait()


def update_call(whole_t, work, cross, trailing):
    rows, width = trailing.shape
    vmem = pl.BlockSpec(memory_space=pltpu.VMEM)
    steps = 8
    return pl.pallas_call(
        update_kernel,
        out_shape=(
            jax.ShapeDtypeStruct((32, 256), F32), jax.ShapeDtypeStruct((256, width), F32),
            jax.ShapeDtypeStruct((rows, width), F32),
        ),
        in_specs=[vmem] * 4,
        out_specs=(vmem, vmem, pl.BlockSpec(memory_space=pl.ANY)),
        scratch_shapes=[
            pltpu.VMEM((256, 256), F32),
            pltpu.VMEM((steps, rows // steps, width), F32),
            pltpu.SemaphoreType.DMA((steps,)),
        ],
        compiler_params=pltpu.CompilerParams(vmem_limit_bytes=40 * 2**20),
    )(whole_t, work, cross, trailing)


def on_device(panel, trailing):
    whole_t, work, cross = panel_call(panel.T, trailing)
    factor_t, coupling, updated = update_call(whole_t, work, cross, trailing)
    return factor_t.T, coupling, updated


def solution(mesh):
    in_specs = (P("row", "col"), P("row", "col"))
    out_specs = (P(None, "col"), P(None, "col"), P("row", "col"))
    return jax.shard_map(
        on_device, mesh=mesh, in_specs=in_specs, out_specs=out_specs, check_vma=False
    )
```

```python
import functools

import jax
import jax.numpy as jnp
from jax import lax
from jax.experimental import pallas as pl
from jax.experimental.pallas import tpu as pltpu
from jax.sharding import PartitionSpec as P

F32 = jnp.float32
BF16 = jnp.bfloat16
HIGHEST = lax.Precision.HIGHEST
MESH = pl.DeviceIdType.MESH
STEP = 32
LANES = 128


def split(value):
    high = value.astype(BF16)
    low = (value - high.astype(F32)).astype(BF16)
    return high, low


def remote(src, dst, send, recv, where):
    return pltpu.make_async_remote_copy(
        src_ref=src, dst_ref=dst, send_sem=send, recv_sem=recv, device_id=where, device_id_type=MESH
    )


def total_of(parts):
    while len(parts) > 1:
        parts = [sum(parts[i : i + 2][1:], parts[i]) for i in range(0, len(parts), 2)]
    return parts[0]


def at(start, size):
    return pl.ds(pl.multiple_of(start * size, size), size)


def panel_kernel(
    pt, tr, high_out, low_out, work, cross_out,
    whole, trail, trail_hi, trail_lo, slab, gram_part, gram_t, gram_p, gram_z, gram_full,
    cross_part, cross_g, cross_z, cross_full,
    loc_sem, ps_s, ps_r, px_s, px_r, sb_s, sb_r, gp_s, gp_r, gz_s, gz_r, gf_s, gf_r,
    tw_s, tw_r, cg_s, cg_r, cz_s, cz_r, cf_s, cf_r, known,
):
    row, col = lax.axis_index("row"), lax.axis_index("col")
    rem, div = lax.rem, lax.div
    z, y = div(row, 4), rem(row, 4)
    x, core = div(col, 2), rem(col, 2)
    zh, zl = div(z, 4), rem(z, 4)
    ys = [y] + [rem(y + d, 4) for d in range(1, 4)]
    cols = [col] + [rem(col + d, 8) for d in range(1, 8)]
    zs = [z] + [rem(z + d, 16) for d in range(1, 16)]
    near = [zl] + [rem(zl + d, 4) for d in range(1, 4)]
    chips = [x] + [rem(x + d, 4) for d in range(1, 4)]

    plane = [(dy, dx) for dy in (2, 1, 3, 0) for dx in (2, 1, 3, 0) if (dy, dx) != (0, 0)]
    block = [(dy, dz) for dz in (2, 1, 3, 0) for dy in (2, 1, 3, 0) if (dy, dz) != (0, 0)]
    line = (8, 7, 9, 6, 10, 5, 11, 4, 12, 3, 13, 2, 14, 1, 15)

    def at_plane(dy, dx):
        return (z * 4 + ys[dy], chips[dx] * 2 + core)

    def at_z(d):
        return (zs[d] * 4 + y, col)

    def at_block(dy, dz):
        return (zh * 16 + near[dz] * 4 + ys[dy], col)

    barrier = pltpu.get_barrier_semaphore()
    for dx in (2, 1, 3, 0):
        where = (row, chips[dx] * 2 + 1 - core)
        pl.semaphore_signal(barrier, inc=1, device_id=where, device_id_type=MESH)
    for dy, dx in plane[::-1]:
        pl.semaphore_signal(barrier, inc=1, device_id=at_plane(dy, dx), device_id_type=MESH)
    for d in (1, 15):
        pl.semaphore_signal(barrier, inc=1, device_id=at_z(d), device_id_type=MESH)
    pl.semaphore_wait(barrier, 21)

    def pass_on(i):
        for d in (2**i, 16 - 2**i):
            pl.semaphore_signal(known.at[i], inc=1, device_id=at_z(d), device_id_type=MESH)

    def slab_copy(d, who):
        return remote(
            pt.at[:, at(cols[d], 256)], slab.at[at(who, 32)], ps_s.at[d], ps_r.at[d], (row, cols[d])
        )

    for d in (4, 3, 5, 2, 6, 1, 7):
        slab_copy(d, col).start()
    slab_own = pltpu.make_async_copy(pt.at[:, at(col, 256)], slab.at[at(col, 32)], loc_sem.at[3])
    slab_own.start()

    half = pt.shape[1] // 2
    right, left = (row, chips[1] * 2 + core), (row, chips[3] * 2 + core)
    twin = (row, x * 2 + 1 - core)

    def slot(far, part):
        return whole.at[at(chips[far] * 2 + core, 32), pl.ds(part * half, half)]

    def own(part):
        return pt.at[:, pl.ds(part * half, half)]

    sends = {
        0: remote(own(0), slot(0, 0), px_s.at[0], px_r.at[0], right),
        1: remote(own(1), slot(0, 1), px_s.at[1], px_r.at[1], left),
        2: remote(own(1), slot(0, 1), px_s.at[2], px_r.at[2], right),
        3: remote(own(0), slot(0, 0), px_s.at[3], px_r.at[3], left),
    }
    for i in range(4):
        sends[i].start()
    to_twin = {}

    def relay(i, far, part, src=None):
        to_twin[i] = remote(
            slot(far, part) if src is None else src, slot(far, part), sb_s.at[i], sb_r.at[i], twin
        )
        to_twin[i].start()

    relay(6, 0, 0, own(0))
    relay(7, 0, 1, own(1))
    panel_own = pltpu.make_async_copy(pt, whole.at[at(col, 32), :], loc_sem.at[0])
    panel_own.start()
    load = pltpu.make_async_copy(tr, trail, loc_sem.at[1])
    load.start()

    pass_on(0)
    load.wait()
    chunk = 256

    @pl.loop(0, pt.shape[1] // chunk)
    def _(i):
        high, low = split(trail[at(i, chunk), :])
        trail_hi[at(i, chunk), :] = high
        trail_lo[at(i, chunk), :] = low

    pl.semaphore_wait(known.at[0], 2)
    pass_on(1)
    slab_own.wait()
    for d in range(1, 8):
        slab_copy(d, cols[8 - d]).wait_recv()
    gram_part[...] = lax.dot_general(
        slab[...], slab[...], (((1,), (1,)), ((), ())), precision=HIGHEST, preferred_element_type=F32
    )
    gram_twin = remote(gram_part.at[at(1 - core, 128)], gram_t, tw_s.at[0], tw_r.at[0], twin)
    gram_twin.start()
    gram_twin.wait_recv()
    gram_t[...] += gram_part[at(core, 128), :]
    place = y * 4 + x
    mine = core * 16 + place

    def gram_p_copy(dy, dx):
        d = dy * 4 + dx
        return remote(
            gram_t.at[at(ys[dy] * 4 + chips[dx], 8)], gram_p.at[d], gp_s.at[d], gp_r.at[d], at_plane(dy, dx)
        )

    for dy, dx in plane:
        gram_p_copy(dy, dx).start()

    pl.semaphore_wait(known.at[1], 2)
    pass_on(2)
    sends[0].wait_recv()
    sends[4] = remote(slot(3, 0), slot(3, 0), px_s.at[4], px_r.at[4], right)
    sends[4].start()
    relay(0, 3, 0)
    sends[1].wait_recv()
    sends[5] = remote(slot(1, 1), slot(1, 1), px_s.at[5], px_r.at[5], left)
    sends[5].start()
    relay(1, 1, 1)

    def cross_g_copy(dy, dz):
        d = dy * 4 + dz
        return remote(
            cross_part.at[at(ys[dy] * 4 + near[dz], 16)], cross_g.at[d], cg_s.at[d], cg_r.at[d], at_block(dy, dz)
        )

    def cross_stage(far):
        rows = at(chips[far], 64)
        high, low = split(whole[rows, :])
        dot = functools.partial(jnp.dot, preferred_element_type=F32)
        cross_part[rows, :] = dot(high, trail_hi[...]) + (
            dot(high, trail_lo[...]) + dot(low, trail_hi[...])
        )
        for dy in range(4):

            @pl.when(ys[dy] == chips[far])
            def _():
                for dz in (2, 1, 3, 0):
                    if dy or dz:
                        cross_g_copy(dy, dz).start()

    panel_own.wait()
    to_twin[6].wait_recv()
    to_twin[7].wait_recv()
    cross_stage(0)
    sends[2].wait_recv()
    relay(2, 3, 1)
    sends[3].wait_recv()
    relay(3, 1, 0)

    for dy, dx in plane:
        gram_p_copy(dy, dx).wait_recv()
    gram_z[z] = total_of([gram_t[at(place, 8), :]] + [gram_p[d] for d in range(1, 16)])

    def gram_z_copy(d, who):
        return remote(gram_z.at[z], gram_z.at[who], gz_s.at[d], gz_r.at[d], at_z(d))

    pl.semaphore_wait(known.at[2], 2)
    for d in line:
        gram_z_copy(d, z).start()

    sends[4].wait_recv()
    relay(4, 2, 0)
    sends[5].wait_recv()
    relay(5, 2, 1)
    for i in range(4):
        to_twin[i].wait_recv()
    cross_stage(1)
    cross_stage(3)
    to_twin[4].wait_recv()
    to_twin[5].wait_recv()
    cross_stage(2)

    group = y * 4 + zl
    for d in range(1, 16):
        gram_z_copy(d, zs[16 - d]).wait_recv()
    gram_full[at(mine, 8), :] = total_of([gram_z[i] for i in range(16)])

    def gram_f_copy(dy, dx, who):
        d = dy * 4 + dx
        return remote(
            gram_full.at[at(mine, 8)], gram_full.at[at(who, 8)], gf_s.at[d], gf_r.at[d], at_plane(dy, dx)
        )

    for dy, dx in plane:
        gram_f_copy(dy, dx, mine).start()

    for dy, dz in block:
        cross_g_copy(dy, dz).wait_recv()
    cross_z[zh] = total_of([cross_part[at(group, 16), :]] + [cross_g[d] for d in range(1, 16)])

    def cross_z_copy(d, who):
        return remote(cross_z.at[zh], cross_z.at[who], cz_s.at[d], cz_r.at[d], at_z(4 * d))

    for d in (2, 1, 3):
        cross_z_copy(d, zh).start()

    @pl.loop(0, pt.shape[1] // chunk)
    def _(i):
        high, low = split(whole[:, at(i, chunk)].T)
        high_out[at(i, chunk), :] = high
        low_out[at(i, chunk), :] = low

    for dy, dx in plane:
        gram_f_copy(dy, dx, core * 16 + ys[-dy] * 4 + chips[-dx]).wait_recv()

    def full_twin(who):
        rows = gram_full.at[at(who, 128)]
        return remote(gram_full.at[at(core, 128)], rows, tw_s.at[1], tw_r.at[1], twin)

    full_twin(core).start()
    full_twin(1 - core).wait_recv()

    def cross_f_copy(dy, dz, who):
        d = dy * 4 + dz
        return remote(
            cross_full.at[at(group, 16)], cross_full.at[at(who, 16)], cf_s.at[d], cf_r.at[d], at_block(dy, dz)
        )

    def share_cross():
        for d in range(1, 4):
            cross_z_copy(d, rem(zh + 4 - d, 4)).wait_recv()
        cross_full[at(group, 16), :] = total_of([cross_z[i] for i in range(4)])
        for dy, dz in block:
            cross_f_copy(dy, dz, group).start()

    factor(gram_full, work, share_cross)

    for dy, dz in block:
        cross_f_copy(dy, dz, ys[-dy] * 4 + near[-dz]).wait_recv()
    cross_out[...] = cross_full[...]

    for i in range(6):
        sends[i].wait_send()
    for i in range(8):
        to_twin[i].wait_send()
    for d in range(1, 4):
        cross_z_copy(d, zh).wait_send()
    for d in range(1, 16):
        gram_z_copy(d, z).wait_send()
    for dy, dz in block:
        cross_g_copy(dy, dz).wait_send()
        cross_f_copy(dy, dz, group).wait_send()
    for d in range(1, 8):
        slab_copy(d, col).wait_send()
    for dy, dx in plane:
        gram_p_copy(dy, dx).wait_send()
        gram_f_copy(dy, dx, mine).wait_send()
    gram_twin.wait_send()
    full_twin(core).wait_send()


def eliminate(rows, lane):
    down = lax.broadcasted_iota(jnp.int32, (STEP, LANES), 0)
    wide = lax.broadcasted_iota(jnp.int32, rows.shape, 0)
    columns = [jnp.broadcast_to(rows[:, lane + j : lane + j + 1], (STEP, LANES)) for j in range(STEP)]

    def across(value):
        return jnp.concatenate([value] * 3, 1)

    for j in range(0, STEP, 2):
        first, second = columns[j][j : j + 1, :], columns[j][j + 1 : j + 2, :]
        third = columns[j + 1][j + 1 : j + 2, :]
        scale_0 = lax.rsqrt(first)
        scale_1 = lax.rsqrt(first * third - second * second) * (first * scale_0)
        link = second * scale_0
        below_0 = jnp.where(down > j, columns[j] * scale_0, 0.0)
        below_1 = jnp.where(down > j + 1, (columns[j + 1] - below_0 * link) * scale_1, 0.0)
        for m in range(j + 2, STEP):
            columns[m] = columns[m] - (below_0 * below_0[m : m + 1, :] + below_1 * below_1[m : m + 1, :])
        row_0 = rows[j : j + 1, :] * across(scale_0)
        row_1 = (rows[j + 1 : j + 2, :] - across(link) * row_0) * across(scale_1)
        rest = rows - (across(below_0) * row_0 + across(below_1) * row_1)
        rows = jnp.where(wide == j, row_0, jnp.where(wide == j + 1, row_1, rest))
    return rows


def factor(gram, work, midway):
    order = gram.shape[0]
    work[...] = jnp.zeros_like(work)

    def span(start):
        return (0, 3 * LANES) if start < LANES else (LANES, 4 * LANES)

    def base(start):
        across = lax.broadcasted_iota(jnp.int32, (STEP, order), 1)
        down = lax.broadcasted_iota(jnp.int32, (STEP, order), 0)
        unit = jnp.where(across == down + start, 1.0, 0.0)
        low, high = span(start)
        return jnp.concatenate([gram[start : start + STEP, :], unit], 1)[:, low:high]

    def terms(start, first, last):
        low, high = span(start)
        return lax.dot_general(
            work[first:last, start : start + STEP], work[first:last, low:high],
            (((0,), (0,)), ((), ())), precision=HIGHEST, preferred_element_type=F32,
        )

    ready = base(0)
    for start in range(0, order, STEP):
        later = start + STEP
        if later < order:
            ahead = base(later)
            if start:
                ahead = ahead - terms(later, 0, start)
        low, high = span(start)
        work[start:later, low:high] = eliminate(ready, start % LANES)
        if start == 0:
            midway()
        if later < order:
            ready = ahead - terms(later, start, later)


def panel_call(pt, trailing):
    dma = pltpu.SemaphoreType.DMA
    rows = pt.shape[1]
    square = jax.ShapeDtypeStruct((256, 256), F32)
    vmem = pl.BlockSpec(memory_space=pltpu.VMEM)
    hbm = pl.BlockSpec(memory_space=pltpu.HBM)
    return pl.pallas_call(
        panel_kernel,
        out_shape=(
            jax.ShapeDtypeStruct((rows, 256), BF16), jax.ShapeDtypeStruct((rows, 256), BF16),
            jax.ShapeDtypeStruct((256, 512), F32), square,
        ),
        in_specs=[hbm, hbm],
        out_specs=(vmem, vmem, vmem, vmem),
        scratch_shapes=[
            pltpu.VMEM((256, rows), F32),
            pltpu.VMEM(trailing.shape, F32),
            pltpu.VMEM(trailing.shape, BF16),
            pltpu.VMEM(trailing.shape, BF16),
            pltpu.VMEM((256, 256), F32),
            pltpu.VMEM((256, 256), F32),
            pltpu.VMEM((128, 256), F32),
            pltpu.VMEM((16, 8, 256), F32),
            pltpu.VMEM((16, 8, 256), F32),
            pltpu.VMEM((256, 256), F32),
            pltpu.VMEM((256, 256), F32),
            pltpu.VMEM((16, 16, 256), F32),
            pltpu.VMEM((4, 16, 256), F32),
            pltpu.VMEM((256, 256), F32),
            dma((4,)), dma((8,)), dma((8,)),
            dma((6,)), dma((6,)), dma((8,)), dma((8,)),
            dma((16,)), dma((16,)), dma((16,)), dma((16,)), dma((16,)), dma((16,)), dma((2,)), dma((2,)),
            dma((16,)), dma((16,)), dma((4,)), dma((4,)), dma((16,)), dma((16,)),
            pltpu.SemaphoreType.REGULAR((3,)),
        ],
        compiler_params=pltpu.CompilerParams(
            collective_id=0, has_side_effects=True, vmem_limit_bytes=40 * 2**20
        ),
    )(pltpu.with_memory_space_constraint(pt, pltpu.HBM), pltpu.with_memory_space_constraint(trailing, pltpu.HBM))


def update_kernel(whole_hi, whole_lo, work, cross, trail, factor_out, coupling_out, updated_out, scratch, block, sems):
    order = work.shape[0]
    upper, lower = work[:, :order], work[:, order:]
    across = lax.broadcasted_iota(jnp.int32, (order, order), 1)
    down = lax.broadcasted_iota(jnp.int32, (order, order), 0)
    coupling = jnp.dot(lower, cross[...], precision=HIGHEST, preferred_element_type=F32)
    coupling_out[...] = coupling
    solved = lax.dot_general(
        lower, coupling, (((0,), (0,)), ((), ())), precision=HIGHEST, preferred_element_type=F32
    )
    solved_hi, solved_lo = split(solved)
    dot = functools.partial(jnp.dot, preferred_element_type=F32)
    steps, size = block.shape[0], block.shape[1]
    copies = []
    for i in range(steps):
        rows = slice(i * size, (i + 1) * size)
        high, low = whole_hi[rows, :], whole_lo[rows, :]
        block[i] = trail[rows, :] - (dot(high, solved_hi) + (dot(high, solved_lo) + dot(low, solved_hi)))
        copies.append(pltpu.make_async_copy(block.at[i], updated_out.at[pl.ds(i * size, size)], sems.at[i]))
        copies[-1].start()
    scratch[...] = jnp.where(across >= down, upper, 0.0).T
    factor_out[...] = scratch[at(lax.axis_index("col"), 32), :]
    for copy in copies:
        copy.wait()


def update_call(whole_hi, whole_lo, work, cross, trailing):
    rows, width = trailing.shape
    vmem = pl.BlockSpec(memory_space=pltpu.VMEM)
    steps = 8
    return pl.pallas_call(
        update_kernel,
        out_shape=(
            jax.ShapeDtypeStruct((32, 256), F32), jax.ShapeDtypeStruct((256, width), F32),
            jax.ShapeDtypeStruct((rows, width), F32),
        ),
        in_specs=[vmem] * 5,
        out_specs=(vmem, vmem, pl.BlockSpec(memory_space=pl.ANY)),
        scratch_shapes=[
            pltpu.VMEM((256, 256), F32),
            pltpu.VMEM((steps, rows // steps, width), F32),
            pltpu.SemaphoreType.DMA((steps,)),
        ],
        compiler_params=pltpu.CompilerParams(vmem_limit_bytes=40 * 2**20),
    )(whole_hi, whole_lo, work, cross, trailing)


def on_device(panel, trailing):
    parts = panel_call(panel.T, trailing)
    factor_t, coupling, updated = update_call(*parts, trailing)
    return factor_t.T, coupling, updated


def solution(mesh):
    in_specs = (P("row", "col"), P("row", "col"))
    out_specs = (P(None, "col"), P(None, "col"), P("row", "col"))
    return jax.shard_map(
        on_device, mesh=mesh, in_specs=in_specs, out_specs=out_specs, check_vma=False
    )
```

```python
import functools

import jax
import jax.numpy as jnp
from jax import lax
from jax.experimental import pallas as pl
from jax.experimental.pallas import tpu as pltpu
from jax.sharding import PartitionSpec as P

F32 = jnp.float32
BF16 = jnp.bfloat16
HIGHEST = lax.Precision.HIGHEST
MESH = pl.DeviceIdType.MESH
STEP = 32
LANES = 128


def split(value):
    high = value.astype(BF16)
    low = (value - high.astype(F32)).astype(BF16)
    return high, low


def dot3(left, right, dims):
    left_hi, left_lo = split(left)
    right_hi, right_lo = split(right)
    dot = functools.partial(
        lax.dot_general, dimension_numbers=(dims, ((), ())), preferred_element_type=F32
    )
    return dot(left_hi, right_hi) + (dot(left_hi, right_lo) + dot(left_lo, right_hi))


def remote(src, dst, send, recv, where):
    return pltpu.make_async_remote_copy(
        src_ref=src, dst_ref=dst, send_sem=send, recv_sem=recv, device_id=where, device_id_type=MESH
    )


def total_of(parts):
    while len(parts) > 1:
        parts = [sum(parts[i : i + 2][1:], parts[i]) for i in range(0, len(parts), 2)]
    return parts[0]


def at(start, size):
    return pl.ds(pl.multiple_of(start * size, size), size)


def panel_kernel(
    pt, tr, high_out, low_out, work, cross_out,
    whole, trail, trail_hi, trail_lo, slab, gram_part, gram_t, gram_p, gram_z, gram_full,
    cross_part, cross_g, cross_z, cross_full,
    loc_sem, ps_s, ps_r, px_s, px_r, sb_s, sb_r, gp_s, gp_r, gz_s, gz_r, gf_s, gf_r,
    tw_s, tw_r, cg_s, cg_r, cz_s, cz_r, cf_s, cf_r, known,
):
    row, col = lax.axis_index("row"), lax.axis_index("col")
    rem, div = lax.rem, lax.div
    z, y = div(row, 4), rem(row, 4)
    x, core = div(col, 2), rem(col, 2)
    zh, zl = div(z, 4), rem(z, 4)
    ys = [y] + [rem(y + d, 4) for d in range(1, 4)]
    cols = [col] + [rem(col + d, 8) for d in range(1, 8)]
    zs = [z] + [rem(z + d, 16) for d in range(1, 16)]
    near = [zl] + [rem(zl + d, 4) for d in range(1, 4)]
    chips = [x] + [rem(x + d, 4) for d in range(1, 4)]

    plane = [(dy, dx) for dy in (2, 1, 3, 0) for dx in (2, 1, 3, 0) if (dy, dx) != (0, 0)]
    block = [(dy, dz) for dz in (2, 1, 3, 0) for dy in (2, 1, 3, 0) if (dy, dz) != (0, 0)]
    line = (8, 7, 9, 6, 10, 5, 11, 4, 12, 3, 13, 2, 14, 1, 15)

    def at_plane(dy, dx):
        return (z * 4 + ys[dy], chips[dx] * 2 + core)

    def at_z(d):
        return (zs[d] * 4 + y, col)

    def at_block(dy, dz):
        return (zh * 16 + near[dz] * 4 + ys[dy], col)

    barrier = pltpu.get_barrier_semaphore()
    for dx in (2, 1, 3, 0):
        where = (row, chips[dx] * 2 + 1 - core)
        pl.semaphore_signal(barrier, inc=1, device_id=where, device_id_type=MESH)
    for dy, dx in plane[::-1]:
        pl.semaphore_signal(barrier, inc=1, device_id=at_plane(dy, dx), device_id_type=MESH)
    for d in (1, 15):
        pl.semaphore_signal(barrier, inc=1, device_id=at_z(d), device_id_type=MESH)
    pl.semaphore_wait(barrier, 21)

    def pass_on(i):
        for d in (2**i, 16 - 2**i):
            pl.semaphore_signal(known.at[i], inc=1, device_id=at_z(d), device_id_type=MESH)

    def slab_copy(d, who):
        return remote(
            pt.at[:, at(cols[d], 256)], slab.at[at(who, 32)], ps_s.at[d], ps_r.at[d], (row, cols[d])
        )

    for d in (4, 3, 5, 2, 6, 1, 7):
        slab_copy(d, col).start()
    slab_own = pltpu.make_async_copy(pt.at[:, at(col, 256)], slab.at[at(col, 32)], loc_sem.at[3])
    slab_own.start()

    half = pt.shape[1] // 2
    right, left = (row, chips[1] * 2 + core), (row, chips[3] * 2 + core)
    twin = (row, x * 2 + 1 - core)

    def slot(far, part):
        return whole.at[at(chips[far] * 2 + core, 32), pl.ds(part * half, half)]

    def own(part):
        return pt.at[:, pl.ds(part * half, half)]

    sends = {
        0: remote(own(0), slot(0, 0), px_s.at[0], px_r.at[0], right),
        1: remote(own(1), slot(0, 1), px_s.at[1], px_r.at[1], left),
        2: remote(own(1), slot(0, 1), px_s.at[2], px_r.at[2], right),
        3: remote(own(0), slot(0, 0), px_s.at[3], px_r.at[3], left),
    }
    to_twin = {}

    def relay(i, far, part, src=None):
        to_twin[i] = remote(
            slot(far, part) if src is None else src, slot(far, part), sb_s.at[i], sb_r.at[i], twin
        )
        to_twin[i].start()

    relay(6, 0, 0, own(0))
    relay(7, 0, 1, own(1))
    panel_own = pltpu.make_async_copy(pt, whole.at[at(col, 32), :], loc_sem.at[0])
    panel_own.start()
    load = pltpu.make_async_copy(tr, trail, loc_sem.at[1])
    load.start()

    pass_on(0)
    for d in range(1, 8):
        slab_copy(d, col).wait_send()
    for i in range(4):
        sends[i].start()
    load.wait()
    chunk = 256

    @pl.loop(0, pt.shape[1] // chunk)
    def _(i):
        high, low = split(trail[at(i, chunk), :])
        trail_hi[at(i, chunk), :] = high
        trail_lo[at(i, chunk), :] = low

    pl.semaphore_wait(known.at[0], 2)
    pass_on(1)
    slab_own.wait()
    for d in range(1, 8):
        slab_copy(d, cols[8 - d]).wait_recv()
    gram_part[...] = lax.dot_general(
        slab[...], slab[...], (((1,), (1,)), ((), ())), precision=HIGHEST, preferred_element_type=F32
    )
    gram_twin = remote(gram_part.at[at(1 - core, 128)], gram_t, tw_s.at[0], tw_r.at[0], twin)
    gram_twin.start()
    gram_twin.wait_recv()
    gram_t[...] += gram_part[at(core, 128), :]
    place = y * 4 + x
    mine = core * 16 + place

    def gram_p_copy(dy, dx):
        d = dy * 4 + dx
        return remote(
            gram_t.at[at(ys[dy] * 4 + chips[dx], 8)], gram_p.at[d], gp_s.at[d], gp_r.at[d], at_plane(dy, dx)
        )

    for dy, dx in plane:
        gram_p_copy(dy, dx).start()

    pl.semaphore_wait(known.at[1], 2)
    pass_on(2)
    sends[0].wait_recv()
    sends[4] = remote(slot(3, 0), slot(3, 0), px_s.at[4], px_r.at[4], right)
    sends[4].start()
    relay(0, 3, 0)
    sends[1].wait_recv()
    sends[5] = remote(slot(1, 1), slot(1, 1), px_s.at[5], px_r.at[5], left)
    sends[5].start()
    relay(1, 1, 1)

    def cross_g_copy(dy, dz):
        d = dy * 4 + dz
        return remote(
            cross_part.at[at(ys[dy] * 4 + near[dz], 16)], cross_g.at[d], cg_s.at[d], cg_r.at[d], at_block(dy, dz)
        )

    def cross_stage(far):
        rows = at(chips[far], 64)
        high, low = split(whole[rows, :])
        dot = functools.partial(jnp.dot, preferred_element_type=F32)
        cross_part[rows, :] = dot(high, trail_hi[...]) + (
            dot(high, trail_lo[...]) + dot(low, trail_hi[...])
        )
        for dy in range(4):

            @pl.when(ys[dy] == chips[far])
            def _():
                for dz in (2, 1, 3, 0):
                    if dy or dz:
                        cross_g_copy(dy, dz).start()

    panel_own.wait()
    to_twin[6].wait_recv()
    to_twin[7].wait_recv()
    cross_stage(0)
    sends[2].wait_recv()
    relay(2, 3, 1)
    sends[3].wait_recv()
    relay(3, 1, 0)

    for dy, dx in plane:
        gram_p_copy(dy, dx).wait_recv()
    gram_z[z] = total_of([gram_t[at(place, 8), :]] + [gram_p[d] for d in range(1, 16)])

    def gram_z_copy(d, who):
        return remote(gram_z.at[z], gram_z.at[who], gz_s.at[d], gz_r.at[d], at_z(d))

    pl.semaphore_wait(known.at[2], 2)
    for d in line:
        gram_z_copy(d, z).start()

    sends[4].wait_recv()
    relay(4, 2, 0)
    sends[5].wait_recv()
    relay(5, 2, 1)
    for i in range(4):
        to_twin[i].wait_recv()
    cross_stage(1)
    cross_stage(3)
    to_twin[4].wait_recv()
    to_twin[5].wait_recv()
    cross_stage(2)

    group = y * 4 + zl
    @pl.loop(0, pt.shape[1] // chunk)
    def _(i):
        high, low = split(whole[:, at(i, chunk)].T)
        high_out[at(i, chunk), :] = high
        low_out[at(i, chunk), :] = low

    for d in range(1, 16):
        gram_z_copy(d, zs[16 - d]).wait_recv()
    gram_full[at(mine, 8), :] = total_of([gram_z[i] for i in range(16)])

    def gram_f_copy(dy, dx, who):
        d = dy * 4 + dx
        return remote(
            gram_full.at[at(mine, 8)], gram_full.at[at(who, 8)], gf_s.at[d], gf_r.at[d], at_plane(dy, dx)
        )

    for dy, dx in plane:
        gram_f_copy(dy, dx, mine).start()

    for dy, dz in block:
        cross_g_copy(dy, dz).wait_recv()
    cross_z[zh] = total_of([cross_part[at(group, 16), :]] + [cross_g[d] for d in range(1, 16)])

    def cross_z_copy(d, who):
        return remote(cross_z.at[zh], cross_z.at[who], cz_s.at[d], cz_r.at[d], at_z(4 * d))

    for d in (2, 1, 3):
        cross_z_copy(d, zh).start()

    for dy, dx in plane:
        gram_f_copy(dy, dx, core * 16 + ys[-dy] * 4 + chips[-dx]).wait_recv()

    def full_twin(who):
        rows = gram_full.at[at(who, 128)]
        return remote(gram_full.at[at(core, 128)], rows, tw_s.at[1], tw_r.at[1], twin)

    full_twin(core).start()
    full_twin(1 - core).wait_recv()

    def cross_f_copy(dy, dz, who):
        d = dy * 4 + dz
        return remote(
            cross_full.at[at(group, 16)], cross_full.at[at(who, 16)], cf_s.at[d], cf_r.at[d], at_block(dy, dz)
        )

    def share_cross():
        for d in range(1, 4):
            cross_z_copy(d, rem(zh + 4 - d, 4)).wait_recv()
        cross_full[at(group, 16), :] = total_of([cross_z[i] for i in range(4)])
        for dy, dz in block:
            cross_f_copy(dy, dz, group).start()

    factor(gram_full, work, share_cross)

    for dy, dz in block:
        cross_f_copy(dy, dz, ys[-dy] * 4 + near[-dz]).wait_recv()
    cross_out[...] = cross_full[...]

    for i in range(6):
        sends[i].wait_send()
    for i in range(8):
        to_twin[i].wait_send()
    for d in range(1, 4):
        cross_z_copy(d, zh).wait_send()
    for d in range(1, 16):
        gram_z_copy(d, z).wait_send()
    for dy, dz in block:
        cross_g_copy(dy, dz).wait_send()
        cross_f_copy(dy, dz, group).wait_send()
    for dy, dx in plane:
        gram_p_copy(dy, dx).wait_send()
        gram_f_copy(dy, dx, mine).wait_send()
    gram_twin.wait_send()
    full_twin(core).wait_send()


def eliminate(rows, lane):
    down = lax.broadcasted_iota(jnp.int32, (STEP, LANES), 0)
    wide = lax.broadcasted_iota(jnp.int32, rows.shape, 0)
    columns = [jnp.broadcast_to(rows[:, lane + j : lane + j + 1], (STEP, LANES)) for j in range(STEP)]

    def across(value):
        return jnp.concatenate([value] * 3, 1)

    for j in range(0, STEP, 2):
        first, second = columns[j][j : j + 1, :], columns[j][j + 1 : j + 2, :]
        third = columns[j + 1][j + 1 : j + 2, :]
        scale_0 = lax.rsqrt(first)
        scale_1 = lax.rsqrt(first * third - second * second) * (first * scale_0)
        link = second * scale_0
        below_0 = jnp.where(down > j, columns[j] * scale_0, 0.0)
        below_1 = jnp.where(down > j + 1, (columns[j + 1] - below_0 * link) * scale_1, 0.0)
        for m in range(j + 2, STEP):
            columns[m] = columns[m] - (below_0 * below_0[m : m + 1, :] + below_1 * below_1[m : m + 1, :])
        row_0 = rows[j : j + 1, :] * across(scale_0)
        row_1 = (rows[j + 1 : j + 2, :] - across(link) * row_0) * across(scale_1)
        rest = rows - (across(below_0) * row_0 + across(below_1) * row_1)
        rows = jnp.where(wide == j, row_0, jnp.where(wide == j + 1, row_1, rest))
    return rows


def factor(gram, work, midway):
    order = gram.shape[0]
    work[...] = jnp.zeros_like(work)

    def span(start):
        return (0, 3 * LANES) if start < LANES else (LANES, 4 * LANES)

    def base(start):
        across = lax.broadcasted_iota(jnp.int32, (STEP, order), 1)
        down = lax.broadcasted_iota(jnp.int32, (STEP, order), 0)
        unit = jnp.where(across == down + start, 1.0, 0.0)
        low, high = span(start)
        return jnp.concatenate([gram[start : start + STEP, :], unit], 1)[:, low:high]

    def terms(start, first, last):
        low, high = span(start)
        return lax.dot_general(
            work[first:last, start : start + STEP], work[first:last, low:high],
            (((0,), (0,)), ((), ())), precision=HIGHEST, preferred_element_type=F32,
        )

    ready = base(0)
    for start in range(0, order, STEP):
        later = start + STEP
        if later < order:
            ahead = base(later)
            if start:
                ahead = ahead - terms(later, 0, start)
        low, high = span(start)
        work[start:later, low:high] = eliminate(ready, start % LANES)
        if start == 0:
            midway()
        if later < order:
            ready = ahead - terms(later, start, later)


def panel_call(pt, trailing):
    dma = pltpu.SemaphoreType.DMA
    rows = pt.shape[1]
    square = jax.ShapeDtypeStruct((256, 256), F32)
    vmem = pl.BlockSpec(memory_space=pltpu.VMEM)
    hbm = pl.BlockSpec(memory_space=pltpu.HBM)
    return pl.pallas_call(
        panel_kernel,
        out_shape=(
            jax.ShapeDtypeStruct((rows, 256), BF16), jax.ShapeDtypeStruct((rows, 256), BF16),
            jax.ShapeDtypeStruct((256, 512), F32), square,
        ),
        in_specs=[hbm, hbm],
        out_specs=(vmem, vmem, vmem, vmem),
        scratch_shapes=[
            pltpu.VMEM((256, rows), F32),
            pltpu.VMEM(trailing.shape, F32),
            pltpu.VMEM(trailing.shape, BF16),
            pltpu.VMEM(trailing.shape, BF16),
            pltpu.VMEM((256, 256), F32),
            pltpu.VMEM((256, 256), F32),
            pltpu.VMEM((128, 256), F32),
            pltpu.VMEM((16, 8, 256), F32),
            pltpu.VMEM((16, 8, 256), F32),
            pltpu.VMEM((256, 256), F32),
            pltpu.VMEM((256, 256), F32),
            pltpu.VMEM((16, 16, 256), F32),
            pltpu.VMEM((4, 16, 256), F32),
            pltpu.VMEM((256, 256), F32),
            dma((4,)), dma((8,)), dma((8,)),
            dma((6,)), dma((6,)), dma((8,)), dma((8,)),
            dma((16,)), dma((16,)), dma((16,)), dma((16,)), dma((16,)), dma((16,)), dma((2,)), dma((2,)),
            dma((16,)), dma((16,)), dma((4,)), dma((4,)), dma((16,)), dma((16,)),
            pltpu.SemaphoreType.REGULAR((3,)),
        ],
        compiler_params=pltpu.CompilerParams(
            collective_id=0, has_side_effects=True, vmem_limit_bytes=40 * 2**20
        ),
    )(pltpu.with_memory_space_constraint(pt, pltpu.HBM), pltpu.with_memory_space_constraint(trailing, pltpu.HBM))


def update_kernel(whole_hi, whole_lo, work, cross, trail, factor_out, coupling_out, updated_out, scratch, block, sems):
    order = work.shape[0]
    upper, lower = work[:, :order], work[:, order:]
    across = lax.broadcasted_iota(jnp.int32, (order, order), 1)
    down = lax.broadcasted_iota(jnp.int32, (order, order), 0)
    coupling = dot3(lower, cross[...], ((1,), (0,)))
    coupling_out[...] = coupling
    solved = dot3(lower, coupling, ((0,), (0,)))
    solved_hi, solved_lo = split(solved)
    dot = functools.partial(jnp.dot, preferred_element_type=F32)
    steps, size = block.shape[0], block.shape[1]
    copies = []
    for i in range(steps):
        rows = slice(i * size, (i + 1) * size)
        high, low = whole_hi[rows, :], whole_lo[rows, :]
        block[i] = trail[rows, :] - (dot(high, solved_hi) + (dot(high, solved_lo) + dot(low, solved_hi)))
        copies.append(pltpu.make_async_copy(block.at[i], updated_out.at[pl.ds(i * size, size)], sems.at[i]))
        copies[-1].start()
    scratch[...] = jnp.where(across >= down, upper, 0.0).T
    factor_out[...] = scratch[at(lax.axis_index("col"), 32), :]
    for copy in copies:
        copy.wait()


def update_call(whole_hi, whole_lo, work, cross, trailing):
    rows, width = trailing.shape
    vmem = pl.BlockSpec(memory_space=pltpu.VMEM)
    steps = 8
    return pl.pallas_call(
        update_kernel,
        out_shape=(
            jax.ShapeDtypeStruct((32, 256), F32), jax.ShapeDtypeStruct((256, width), F32),
            jax.ShapeDtypeStruct((rows, width), F32),
        ),
        in_specs=[vmem] * 5,
        out_specs=(vmem, vmem, pl.BlockSpec(memory_space=pl.ANY)),
        scratch_shapes=[
            pltpu.VMEM((256, 256), F32),
            pltpu.VMEM((steps, rows // steps, width), F32),
            pltpu.SemaphoreType.DMA((steps,)),
        ],
        compiler_params=pltpu.CompilerParams(vmem_limit_bytes=40 * 2**20),
    )(whole_hi, whole_lo, work, cross, trailing)


def on_device(panel, trailing):
    parts = panel_call(panel.T, trailing)
    factor_t, coupling, updated = update_call(*parts, trailing)
    return factor_t.T, coupling, updated


def solution(mesh):
    in_specs = (P("row", "col"), P("row", "col"))
    out_specs = (P(None, "col"), P(None, "col"), P("row", "col"))
    return jax.shard_map(
        on_device, mesh=mesh, in_specs=in_specs, out_specs=out_specs, check_vma=False
    )
```
